32 devices in a mesh: grp: 2 (over y), gx: 4 (over z), gy: 4 (over x, core).
Axes of the slice: x: 2, y: 2, z: 4, core: 2. Of those that a mesh axis runs over, the one named last changes fastest.
Arguments:
- plane_input: bfloat16 [64, 256, 2048], P(None, ('grp', 'gx'), 'gy'), parts along dimension 1, may hold values from -6 to 6
- row_weight: bfloat16 [2, 16, 64, 64], replicated, may hold values from -0.75 to 0.75
- col_weight: bfloat16 [2, 16, 64, 64], replicated, may hold values from -0.75 to 0.75
- skip_weight: bfloat16 [64, 64], replicated, may hold values from -0.75 to 0.75
- up_weight: bfloat16 [64, 256], replicated, may hold values from -0.03491211 to 0.03491211
- up_bias: float32 [256], replicated, may hold values from -3 to -2
- down_weight: bfloat16 [256, 64], replicated, may hold values from -1.5 to 1.5
- down_bias: float32 [64], replicated, may hold values from -0.15 to 0.15
Outputs:
- output: bfloat16 [64, 256, 2048], P(None, ('grp', 'gx'), 'gy'), parts along dimension 1
The draws below stay inside these ranges and needn't reach their ends.
There are 2 independent parts, one for each index of `grp`. The reference program is written for one: setup_inputs(seed, part) draws one part's arguments, and reference() takes and returns one part's arrays. A program takes and returns all parts, laid end to end along the dimension named above; an argument that names none is the same for every part. Nothing has to cross between parts.
All inputs are finite; a program needn't handle non-finite values.
Results may differ from the reference program's by a relative error of at most 0.0066.
Values may be sent and summed in bfloat16 or wider, within the bound.
No kernel may reach another device: no remote copies, remote signals or barrier semaphores. Data moves between devices by JAX's collectives and lax.ppermute only.
A program may use at most 128 MiB of HBM per device.

```python
import math
import jax
import jax.numpy as jnp
from jax import lax

C = 64
MODES = 16
HIDDEN_SIZE = 256
CX = 32
NX = 128
NY = 2048


def level_of(rng, dims, shards, smallest, largest):
    gain, own = 1.0, jax.random.fold_in(rng, 6)
    for axis_at, parts in shards:
        draws = jnp.exp(jax.random.uniform(jax.random.fold_in(own, axis_at), (parts,), jnp.float32, smallest / len(shards), largest / len(shards)))
        gain = gain * jnp.repeat(draws, dims[axis_at] // parts).reshape([-1 if axis == axis_at else 1 for axis in range(len(dims))])
    return gain


def normal_values(stream_key, extent, scale, most, shards=(), kind=jnp.bfloat16):
    drawn = scale * jax.random.normal(stream_key, extent, jnp.float32)
    if shards:
        drawn = drawn * level_of(stream_key, extent, shards, -0.22, 0.18)
    return jnp.clip(drawn, -most, most).astype(kind)


def setup_inputs(seed: int = 0, part: int = 0) -> dict:
    streams_of = jax.random.split(jax.random.key(seed), 9)
    own_keys = jax.random.split(jax.random.fold_in(streams_of[8], part), 9)
    plane_input = normal_values(own_keys[0], (C, NX, NY), 1.0, 6.0, ((1, 4), (2, 4)))
    row_weight = normal_values(streams_of[1], (2, MODES, C, C), C ** -0.5, 0.75)
    col_weight = normal_values(streams_of[2], (2, MODES, C, C), C ** -0.5, 0.75)
    skip_weight = normal_values(streams_of[3], (C, C), C ** -0.5, 0.75)
    up_weight = jnp.clip(jax.random.uniform(streams_of[4], (C, HIDDEN_SIZE), jnp.float32, -0.03491211, 0.03491211), -0.03491211, 0.03491211).astype(jnp.bfloat16)
    up_bias = jnp.clip(jax.random.uniform(streams_of[5], (HIDDEN_SIZE,), jnp.float32, -3.0, -2.0), -3.0, -2.0)
    down_weight = jnp.clip(jax.random.uniform(streams_of[6], (HIDDEN_SIZE, C), jnp.float32, -1.5, 1.5), -1.5, 1.5).astype(jnp.bfloat16)
    down_bias = jnp.clip(jax.random.uniform(streams_of[7], (C,), jnp.float32, -0.15, 0.15), -0.15, 0.15)
    return {"plane_input": plane_input, "row_weight": row_weight, "col_weight": col_weight, "skip_weight": skip_weight, "up_weight": up_weight, "up_bias": up_bias, "down_weight": down_weight, "down_bias": down_bias}


def forward_table(mode_count, period, offset, number):
    wave_index = jnp.arange(mode_count, dtype=jnp.int32)
    cell_index = offset + jnp.arange(number, dtype=jnp.int32)
    phases = (wave_index[:, None] * cell_index[None, :]) % period
    angles = phases.astype(jnp.float32) * (2.0 * math.pi / period)
    return jnp.concatenate([jnp.cos(angles), -jnp.sin(angles)], axis=0).astype(jnp.bfloat16)


def inverse_table(mode_count, period, offset, number):
    wave_index = jnp.arange(mode_count, dtype=jnp.int32)
    cell_index = offset + jnp.arange(number, dtype=jnp.int32)
    phases = (cell_index[:, None] * wave_index[None, :]) % period
    angles = phases.astype(jnp.float32) * (2.0 * math.pi / period)
    factors = jnp.where(wave_index == 0, 1.0, 2.0).astype(jnp.float32)[None, :]
    return jnp.concatenate([factors * jnp.cos(angles), -factors * jnp.sin(angles)], axis=1).astype(jnp.bfloat16)


def mix_rows(spectrum, weight):
    mode_count = weight.shape[1]
    highest = lax.Precision.HIGHEST
    real_part = spectrum[:, :mode_count]
    imag_part = spectrum[:, mode_count:]
    w_real = weight[0].astype(jnp.float32)
    w_imag = weight[1].astype(jnp.float32)
    first = jnp.einsum('cky,kco->oky', real_part, w_real, precision=highest) - jnp.einsum('cky,kco->oky', imag_part, w_imag, precision=highest)
    second = jnp.einsum('cky,kco->oky', imag_part, w_real, precision=highest) + jnp.einsum('cky,kco->oky', real_part, w_imag, precision=highest)
    return jnp.concatenate([first, second], axis=1).astype(jnp.bfloat16)


def mix_cols(spectrum, weight):
    mode_count = weight.shape[1]
    highest = lax.Precision.HIGHEST
    real_part = spectrum[:, :, :mode_count]
    imag_part = spectrum[:, :, mode_count:]
    w_real = weight[0].astype(jnp.float32)
    w_imag = weight[1].astype(jnp.float32)
    first = jnp.einsum('cxk,kco->oxk', real_part, w_real, precision=highest) - jnp.einsum('cxk,kco->oxk', imag_part, w_imag, precision=highest)
    second = jnp.einsum('cxk,kco->oxk', imag_part, w_real, precision=highest) + jnp.einsum('cxk,kco->oxk', real_part, w_imag, precision=highest)
    return jnp.concatenate([first, second], axis=2).astype(jnp.bfloat16)


def reference(plane_input, row_weight, col_weight, skip_weight, up_weight, up_bias, down_weight, down_bias):
    highest = lax.Precision.HIGHEST
    block_count = NX // CX
    col_forward = forward_table(MODES, NY, 0, NY).astype(jnp.float32)
    col_inverse = inverse_table(MODES, NY, 0, NY).astype(jnp.float32)
    row_scale = float(NX * MODES) ** -0.5
    col_scale = float(NY * MODES) ** -0.5

    def spectra_step(total, block):
        rows = lax.dynamic_slice_in_dim(plane_input, block * CX, CX, 1).astype(jnp.float32)
        row_forward = forward_table(MODES, NX, block * CX, CX).astype(jnp.float32)
        total = total + jnp.einsum('cxy,jx->cjy', rows, row_forward, precision=highest)
        col_part = jnp.einsum('cxy,jy->cxj', rows, col_forward, precision=highest)
        return total, col_part

    start_total = jnp.zeros((C, 2 * MODES, NY), jnp.float32)
    blocks = jnp.arange(block_count, dtype=jnp.int32)
    row_spectrum, col_blocks = lax.scan(spectra_step, start_total, blocks)
    col_spectrum = col_blocks.transpose(1, 0, 2, 3).reshape(C, NX, 2 * MODES)
    row_mixed = mix_rows(row_spectrum, row_weight).astype(jnp.float32)
    col_mixed = mix_cols(col_spectrum, col_weight)
    skip_float = skip_weight.astype(jnp.float32)
    up_float = up_weight.astype(jnp.float32)
    down_float = down_weight.astype(jnp.float32)

    def output_block(block):
        rows = lax.dynamic_slice_in_dim(plane_input, block * CX, CX, 1).astype(jnp.float32)
        row_inverse = inverse_table(MODES, NX, block * CX, CX).astype(jnp.float32)
        from_rows = jnp.einsum('ojy,xj->oxy', row_mixed, row_inverse, precision=highest) * row_scale
        col_rows = lax.dynamic_slice_in_dim(col_mixed, block * CX, CX, 1).astype(jnp.float32)
        from_cols = jnp.einsum('oxj,yj->oxy', col_rows, col_inverse, precision=highest) * col_scale
        local = jnp.einsum('cxy,co->oxy', rows, skip_float, precision=highest)
        rounded = lax.optimization_barrier((from_rows + from_cols + local).astype(jnp.bfloat16))
        mixed_input = rounded.astype(jnp.float32)
        hidden_pre = jnp.einsum('cxy,ch->hxy', mixed_input, up_float, precision=highest) + up_bias[:, None, None]
        hidden_low = lax.optimization_barrier(jax.nn.gelu(hidden_pre, approximate=False).astype(jnp.bfloat16))
        hidden = hidden_low.astype(jnp.float32)
        result = jnp.einsum('hxy,ho->oxy', hidden, down_float, precision=highest) + down_bias[:, None, None]
        return result.astype(jnp.bfloat16)

    pieces = lax.map(output_block, blocks)
    return pieces.transpose(1, 0, 2, 3).reshape(C, NX, NY)
```

```python
import math

import jax
import jax.numpy as jnp
import numpy as np
from jax import lax
from jax.experimental import pallas as pl
from jax.experimental.pallas import tpu as pltpu
from jax.sharding import PartitionSpec as P

LANES = 128
GROUP = 16
HALF_GROUP = 8
BIAS_ROWS = 16
TILE = 512
VMEM_BYTES = 48 * 1024 * 1024
HEAD_VMEM_BYTES = 63 * 1024 * 1024

TAIL = 0.4
COEFFS = (0.15957266, 0.16051476, 0.12055834, 0.14408696, -0.08478078)
EXP_SCALE = -0.5 * math.log2(math.e)


def gelu(v):
    t = jnp.abs(v)
    s = 1.0 / (1.0 + TAIL * t)
    poly = COEFFS[-1]
    for c in COEFFS[-2::-1]:
        poly = poly * s + c
    return jnp.maximum(v, 0.0) - jnp.exp2(t * t * EXP_SCALE) * (poly * s) * t


def row_tables(mode_count, shares, row_count):
    period = shares * row_count
    phases = np.arange(mode_count)[:, None] * np.arange(period)[None, :] % period
    angles = phases.astype(np.float64) * (2.0 * math.pi / period)
    table = np.stack([np.cos(angles), -np.sin(angles)], axis=1).reshape(2 * mode_count, shares, row_count)
    eye = np.eye(HALF_GROUP)
    whole = np.einsum("jsx,cd->sjcdx", table, eye)
    return jnp.asarray(
        whole.reshape(shares, 2 * mode_count * HALF_GROUP, HALF_GROUP * row_count), jnp.bfloat16
    )


def row_inverse_tables(mode_count, shares, row_count):
    period = shares * row_count
    phases = np.arange(period)[:, None] * np.arange(mode_count)[None, :] % period
    angles = phases.astype(np.float64) * (2.0 * math.pi / period)
    factors = np.where(np.arange(mode_count) == 0, 1.0, 2.0)
    table = np.stack([factors * np.cos(angles), -factors * np.sin(angles)], axis=2)
    table = table.reshape(shares, row_count, 2 * mode_count)
    whole = np.einsum("sxj,cd->sxcjd", table, np.eye(GROUP))
    return jnp.asarray(
        whole.reshape(shares, row_count * GROUP, 2 * mode_count * GROUP), jnp.bfloat16
    )


def forward_table(mode_count, period, offset, number):
    wave_index = jnp.arange(mode_count, dtype=jnp.int32)
    cell_index = offset + jnp.arange(number, dtype=jnp.int32)
    phases = wave_index[:, None] * cell_index[None, :] % period
    angles = phases.astype(jnp.float32) * (2.0 * math.pi / period)
    both = jnp.stack([jnp.cos(angles), -jnp.sin(angles)], axis=1)
    return both.reshape(2 * mode_count, number).astype(jnp.bfloat16)


def inverse_table(mode_count, period, offset, number):
    wave_index = jnp.arange(mode_count, dtype=jnp.int32)
    cell_index = offset + jnp.arange(number, dtype=jnp.int32)
    phases = wave_index[:, None] * cell_index[None, :] % period
    angles = phases.astype(jnp.float32) * (2.0 * math.pi / period)
    factors = jnp.where(wave_index == 0, 1.0, 2.0).astype(jnp.float32)[:, None]
    both = jnp.stack([factors * jnp.cos(angles), -factors * jnp.sin(angles)], axis=1)
    return both.reshape(2 * mode_count, number).astype(jnp.bfloat16)


def mix_kernel(row_ref, col_ref, row_out_ref, col_out_ref):
    for source, target in ((row_ref, row_out_ref), (col_ref, col_out_ref)):
        for k in range(source.shape[1]):
            real = source[0, k].astype(jnp.float32).T
            imag = source[1, k].astype(jnp.float32).T
            upper = jnp.concatenate([real, -imag], axis=1)
            lower = jnp.concatenate([imag, real], axis=1)
            target[k] = jnp.concatenate([upper, lower], axis=0).astype(jnp.bfloat16)


def mix_matrices(row_weight, col_weight):
    _, modes, channels, _ = row_weight.shape
    shape = jax.ShapeDtypeStruct((modes, 2 * channels, 2 * channels), jnp.bfloat16)
    return pl.pallas_call(
        mix_kernel,
        out_shape=(shape, shape),
        compiler_params=pltpu.CompilerParams(vmem_limit_bytes=VMEM_BYTES),
        cost_estimate=pl.CostEstimate(flops=10**8, bytes_accessed=2 * 2**20, transcendentals=0),
        name="mix_matrices",
    )(row_weight, col_weight)


def row_modes_kernel(place_ref, table_ref, send_in_ref, keep_in_ref, send_ref, keep_ref):
    table = table_ref[0]
    for source, target in ((send_in_ref, send_ref), (keep_in_ref, keep_ref)):
        parts = []
        for half in range(2):
            block = source[half * HALF_GROUP : (half + 1) * HALF_GROUP]
            block = block.reshape(-1, LANES)
            modes = jnp.dot(table, block, preferred_element_type=jnp.float32)
            parts.append(modes.reshape(-1, HALF_GROUP, LANES))
        target[...] = jnp.concatenate(parts, axis=1).astype(jnp.bfloat16)


def row_modes(place, tables, plane, mode_count):
    channels, row_count, _ = plane.shape
    shape = jax.ShapeDtypeStruct((2 * mode_count, channels, LANES), jnp.bfloat16)
    block = pl.BlockSpec((2 * mode_count, GROUP, LANES), lambda g, place: (0, g, 0))
    return pl.pallas_call(
        row_modes_kernel,
        out_shape=(shape, shape),
        grid_spec=pltpu.PrefetchScalarGridSpec(
            num_scalar_prefetch=1,
            grid=(channels // GROUP,),
            in_specs=[
                pl.BlockSpec((1,) + tables.shape[1:], lambda g, place: (place[2], 0, 0)),
                pl.BlockSpec((GROUP, row_count, LANES), lambda g, place: (g, 0, place[1])),
                pl.BlockSpec((GROUP, row_count, LANES), lambda g, place: (g, 0, place[0])),
            ],
            out_specs=(block, block),
        ),
        compiler_params=pltpu.CompilerParams(vmem_limit_bytes=HEAD_VMEM_BYTES),
        cost_estimate=pl.CostEstimate(flops=2 * 10**9, bytes_accessed=3 * 2**20, transcendentals=0),
        name="row_modes",
    )(place, tables, plane, plane)


def col_modes_kernel(table_ref, plane_ref, out_ref):
    block = plane_ref[...].reshape(-1, plane_ref.shape[2])
    out_ref[...] = lax.dot_general(
        table_ref[...], block, (((1,), (1,)), ((), ())), preferred_element_type=jnp.float32
    )


def col_modes(table, plane):
    channels, row_count, col_count = plane.shape
    modes = table.shape[0]
    return pl.pallas_call(
        col_modes_kernel,
        out_shape=jax.ShapeDtypeStruct((modes, channels * row_count), jnp.float32),
        grid=(channels // GROUP,),
        in_specs=[
            pl.BlockSpec((modes, col_count), lambda g: (0, 0)),
            pl.BlockSpec((GROUP, row_count, col_count), lambda g: (g, 0, 0)),
        ],
        out_specs=pl.BlockSpec((modes, GROUP * row_count), lambda g: (0, g)),
        compiler_params=pltpu.CompilerParams(vmem_limit_bytes=VMEM_BYTES),
        cost_estimate=pl.CostEstimate(flops=10**9, bytes_accessed=3 * 2**20, transcendentals=0),
        name="col_modes",
    )(table, plane)


def finish_kernel(
    row_scale,
    place_ref,
    modes_ref,
    mix_ref,
    inverse_ref,
    local_ref,
    plane_ref,
    col_ref,
    up_ref,
    down_ref,
    down_bias_ref,
    order_ref,
    *rest,
):
    out_ref, mixed_ref, pre_ref, done_ref, wide_ref = rest[-5:]
    mode_rows, channels, _ = modes_ref.shape
    row_count = plane_ref.shape[0]
    for k in range(mode_rows // 2):
        pair = modes_ref[2 * k : 2 * k + 2].reshape(2 * channels, LANES)
        mixed = jnp.dot(mix_ref[k], pair, preferred_element_type=jnp.float32) * row_scale
        mixed_ref[2 * k : 2 * k + 2] = mixed.astype(jnp.bfloat16).reshape(2, channels, LANES)
    for g in range(channels // GROUP):
        part = mixed_ref[:, g * GROUP : (g + 1) * GROUP, :].reshape(mode_rows * GROUP, LANES)
        rows = jnp.dot(inverse_ref[0], part, preferred_element_type=jnp.float32)
        pre_ref[:, g * GROUP : (g + 1) * GROUP, :] = rows.reshape(row_count, GROUP, LANES)
    cols = col_ref[...]

    def one_row(x):
        data = jnp.concatenate([plane_ref[x], cols], axis=0)
        local = jnp.dot(local_ref[x], data, preferred_element_type=jnp.float32)
        return (pre_ref[x] + local).astype(jnp.bfloat16)

    def gather(x, carry):
        at = pl.ds(pl.multiple_of(x * LANES, LANES), LANES)
        wide_ref[:channels, at] = one_row(x)
        return carry

    lax.fori_loop(0, row_count, gather, 0, unroll=32)
    wide_ref[channels:, :] = jnp.ones((BIAS_ROWS, wide_ref.shape[1]), jnp.bfloat16)
    bias = down_bias_ref[...]
    tiles = wide_ref.shape[1] // TILE

    def up(i):
        return jnp.dot(up_ref[...], wide_ref[:, i * TILE : (i + 1) * TILE], preferred_element_type=jnp.float32)

    def down(i, hidden):
        out = jnp.dot(down_ref[...], hidden, preferred_element_type=jnp.float32)
        for q in range(TILE // LANES):
            done_ref[i * (TILE // LANES) + q] = (out[:, q * LANES : (q + 1) * LANES] + bias).astype(jnp.bfloat16)

    waiting = up(0)
    hidden = None
    for i in range(tiles):
        following = up(i + 1) if i + 1 < tiles else None
        active = gelu(waiting).astype(jnp.bfloat16)
        if hidden is not None:
            down(i - 1, hidden)
        hidden, waiting = active, following
    down(tiles - 1, hidden)
    for g in range(channels // GROUP):
        for h in range(row_count // GROUP):
            o, x = slice(g * GROUP, (g + 1) * GROUP), slice(h * GROUP, (h + 1) * GROUP)
            block = done_ref[x, o, :].reshape(GROUP * GROUP, LANES)
            turned = jnp.dot(order_ref[...], block, preferred_element_type=jnp.float32)
            out_ref[o, x, :] = turned.astype(jnp.bfloat16).reshape(GROUP, GROUP, LANES)


def finish(place, which, modes, shared, plane_rows, col_inverse, row_scale, out):
    mix, inverse, local, up, down, down_bias, order = shared
    row_count, channels, col_count = plane_rows.shape

    def whole(a):
        return pl.BlockSpec(a.shape, lambda i, place: (0,) * a.ndim)

    operands = [modes, mix, inverse, local, plane_rows, col_inverse, up, down, down_bias, order]
    in_specs = [
        whole(modes),
        whole(mix),
        pl.BlockSpec((1,) + inverse.shape[1:], lambda i, place: (place[2], 0, 0)),
        whole(local),
        pl.BlockSpec((row_count, channels, LANES), lambda i, place: (0, 0, place[which])),
        pl.BlockSpec((col_inverse.shape[0], LANES), lambda i, place: (0, place[which])),
        whole(up),
        whole(down),
        whole(down_bias),
        whole(order),
    ]
    aliases = {}
    if out is not None:
        operands.append(out)
        in_specs.append(pl.BlockSpec(memory_space=pl.ANY))
        aliases = {len(operands): 0}

    def kernel(*refs):
        finish_kernel(row_scale, *refs)

    return pl.pallas_call(
        kernel,
        out_shape=jax.ShapeDtypeStruct((channels, row_count, col_count), jnp.bfloat16),
        grid_spec=pltpu.PrefetchScalarGridSpec(
            num_scalar_prefetch=1,
            grid=(1,),
            in_specs=in_specs,
            out_specs=pl.BlockSpec((channels, row_count, LANES), lambda i, place: (0, 0, place[which])),
            scratch_shapes=[
                pltpu.VMEM(modes.shape, jnp.bfloat16),
                pltpu.VMEM((row_count, channels, LANES), jnp.float32),
                pltpu.VMEM((row_count, channels, LANES), jnp.bfloat16),
                pltpu.VMEM((channels+BIAS_ROWS, row_count * LANES), jnp.bfloat16),
            ],
        ),
        input_output_aliases=aliases,
        compiler_params=pltpu.CompilerParams(vmem_limit_bytes=VMEM_BYTES),
        cost_estimate=pl.CostEstimate(flops=5 * 10**9, bytes_accessed=4 * 2**20, transcendentals=2 * 10**6),
        name="finish",
    )(place, *operands)


def add(a, b):
    return (a.astype(jnp.float32) + b.astype(jnp.float32)).astype(jnp.bfloat16)


NEAR = [(0, 1), (1, 0), (2, 3), (3, 2)]
FAR = [(0, 3), (3, 0), (1, 2), (2, 1)]


def sum_over_cols_axis(value):
    size = lax.axis_size("gy")
    if size & (size - 1):
        return lax.psum(value, "gy")
    step = 1
    while step < size:
        value = value + lax.ppermute(value, "gy", [(i, i ^ step) for i in range(size)])
        step *= 2
    return value


def body(
    plane_input, row_weight, col_weight, skip_weight, up_weight, up_bias, down_weight, down_bias
):
    channels, row_count, col_count = plane_input.shape
    mode_count = row_weight.shape[1]
    shares = lax.axis_size("gx")
    row_total = row_count * shares
    col_total = col_count * lax.axis_size("gy")
    row_scale = float(row_total * mode_count) ** (-0.5)
    col_scale = float(col_total * mode_count) ** (-0.5)
    share = lax.axis_index("gx")
    line = shares == 4
    inner = jnp.where((share == 1) | (share == 2), 1, 0) if line else jnp.zeros((), jnp.int32)
    rounds = col_count // (2 * LANES)
    places = [
        jnp.stack([2 * r + inner, 2 * r + 1 - inner, share]).astype(jnp.int32) for r in range(rounds)
    ]
    tables = row_tables(mode_count, shares, row_count)

    partial = [row_modes(places[r], tables, plane_input, mode_count) for r in range(rounds)]
    if line:
        near = [lax.ppermute(send, "gx", NEAR) for send, _ in partial]
        half = [add(keep, got) for (_, keep), got in zip(partial, near)]
        far = [lax.ppermute(value, "gx", FAR) for value in half]
        own = [add(value, got) for value, got in zip(half, far)]
        other = [lax.ppermute(value, "gx", NEAR) for value in own]
    else:
        own = [lax.psum(keep.astype(jnp.float32), "gx").astype(jnp.bfloat16) for _, keep in partial]
        other = [lax.psum(send.astype(jnp.float32), "gx").astype(jnp.bfloat16) for send, _ in partial]

    row_mix, col_mix = mix_matrices(row_weight, col_weight)
    col_offset = lax.axis_index("gy") * col_count
    col_partial = col_modes(forward_table(mode_count, col_total, col_offset, col_count), plane_input)
    col_spectrum = sum_over_cols_axis(col_partial)
    col_spectrum = col_spectrum.astype(jnp.bfloat16).reshape(mode_count, 2 * channels, row_count)
    col_mixed = jnp.einsum(
        "koc,kcx->kox", col_mix, col_spectrum, preferred_element_type=jnp.float32
    )
    col_mixed = (col_mixed * col_scale).astype(jnp.bfloat16)
    col_mixed = col_mixed.reshape(2 * mode_count, channels, row_count).transpose(2, 1, 0)
    skip = jnp.broadcast_to(skip_weight.T[None], (row_count, channels, channels))
    local = jnp.concatenate([skip, col_mixed], axis=2)
    col_inverse = inverse_table(mode_count, col_total, col_offset, col_count)
    high = lax.reduce_precision(up_bias, 8, 7)
    middle = lax.reduce_precision(up_bias - high, 8, 7)
    low = up_bias - high - middle
    bias_part = jnp.pad(jnp.stack([high, middle, low], axis=1), ((0, 0), (0, BIAS_ROWS - 3)))
    bias_part = bias_part.astype(jnp.bfloat16)
    up = jnp.concatenate([up_weight.T, bias_part], axis=1)
    order = np.zeros((GROUP, GROUP, GROUP, GROUP), np.float32)
    for a in range(GROUP):
        for b in range(GROUP):
            order[a, b, b, a] = 1.0
    order = jnp.asarray(order.reshape(GROUP * GROUP, GROUP * GROUP), jnp.bfloat16)
    shared = (
        row_mix,
        row_inverse_tables(mode_count, shares, row_count),
        local,
        up,
        down_weight.T,
        jnp.broadcast_to(down_bias[:, None], (channels, LANES)),
        order,
    )
    plane_rows = plane_input.transpose(1, 0, 2)
    out = None
    for r in range(rounds):
        for which, modes in ((0, own[r]), (1, other[r])):
            out = finish(places[r], which, modes, shared, plane_rows, col_inverse, row_scale, out)
    return out


def solution(mesh):
    placed = (P(None, ("grp", "gx"), "gy"), P(), P(), P(), P(), P(), P(), P())
    return jax.shard_map(
        body, mesh=mesh, in_specs=placed, out_specs=P(None, ("grp", "gx"), "gy"), check_vma=False
    )
```

```python
import math

import jax
import jax.numpy as jnp
import numpy as np
from jax import lax
from jax.experimental import pallas as pl
from jax.experimental.pallas import tpu as pltpu
from jax.sharding import PartitionSpec as P

LANES = 128
GROUP = 16
HALF_GROUP = 8
BIAS_ROWS = 16
STEP_CHANNELS = 32
TILE = 512
VMEM_BYTES = 24 * 1024 * 1024
HEAD_VMEM_BYTES = 63 * 1024 * 1024

TAIL = 0.4
COEFFS = (0.15957266, 0.16051476, 0.12055834, 0.14408696, -0.08478078)
EXP_SCALE = -0.5 * math.log2(math.e)


def gelu(v):
    t = jnp.abs(v)
    s = 1.0 / (1.0 + TAIL * t)
    poly = COEFFS[-1]
    for c in COEFFS[-2::-1]:
        poly = poly * s + c
    return jnp.maximum(v, 0.0) - jnp.exp2(t * t * EXP_SCALE) * (poly * s) * t


def row_tables(mode_count, shares, row_count):
    period = shares * row_count
    phases = np.arange(mode_count)[:, None] * np.arange(period)[None, :] % period
    angles = phases.astype(np.float64) * (2.0 * math.pi / period)
    table = np.stack([np.cos(angles), -np.sin(angles)], axis=1).reshape(2 * mode_count, shares, row_count)
    eye = np.eye(HALF_GROUP)
    whole = np.einsum("jsx,cd->sjcdx", table, eye)
    return jnp.asarray(
        whole.reshape(shares, 2 * mode_count * HALF_GROUP, HALF_GROUP * row_count), jnp.bfloat16
    )


def row_inverse_tables(mode_count, shares, row_count):
    period = shares * row_count
    phases = np.arange(period)[:, None] * np.arange(mode_count)[None, :] % period
    angles = phases.astype(np.float64) * (2.0 * math.pi / period)
    factors = np.where(np.arange(mode_count) == 0, 1.0, 2.0)
    table = np.stack([factors * np.cos(angles), -factors * np.sin(angles)], axis=2)
    table = table.reshape(shares, row_count, 2 * mode_count)
    whole = np.einsum("sxj,cd->sxcjd", table, np.eye(GROUP))
    return jnp.asarray(
        whole.reshape(shares, row_count * GROUP, 2 * mode_count * GROUP), jnp.bfloat16
    )


def forward_table(mode_count, period, offset, number):
    wave_index = jnp.arange(mode_count, dtype=jnp.int32)
    cell_index = offset + jnp.arange(number, dtype=jnp.int32)
    phases = wave_index[:, None] * cell_index[None, :] % period
    angles = phases.astype(jnp.float32) * (2.0 * math.pi / period)
    both = jnp.stack([jnp.cos(angles), -jnp.sin(angles)], axis=1)
    return both.reshape(2 * mode_count, number).astype(jnp.bfloat16)


def inverse_table(mode_count, period, offset, number):
    wave_index = jnp.arange(mode_count, dtype=jnp.int32)
    cell_index = offset + jnp.arange(number, dtype=jnp.int32)
    phases = wave_index[:, None] * cell_index[None, :] % period
    angles = phases.astype(jnp.float32) * (2.0 * math.pi / period)
    factors = jnp.where(wave_index == 0, 1.0, 2.0).astype(jnp.float32)[:, None]
    both = jnp.stack([factors * jnp.cos(angles), -factors * jnp.sin(angles)], axis=1)
    return both.reshape(2 * mode_count, number).astype(jnp.bfloat16)


def mix_kernel(row_ref, col_ref, row_out_ref, col_out_ref):
    for source, target in ((row_ref, row_out_ref), (col_ref, col_out_ref)):
        for k in range(source.shape[1]):
            real = source[0, k].astype(jnp.float32).T
            imag = source[1, k].astype(jnp.float32).T
            upper = jnp.concatenate([real, -imag], axis=1)
            lower = jnp.concatenate([imag, real], axis=1)
            target[k] = jnp.concatenate([upper, lower], axis=0).astype(jnp.bfloat16)


def mix_matrices(row_weight, col_weight):
    _, modes, channels, _ = row_weight.shape
    shape = jax.ShapeDtypeStruct((modes, 2 * channels, 2 * channels), jnp.bfloat16)
    return pl.pallas_call(
        mix_kernel,
        out_shape=(shape, shape),
        compiler_params=pltpu.CompilerParams(vmem_limit_bytes=VMEM_BYTES),
        cost_estimate=pl.CostEstimate(flops=0, bytes_accessed=0, transcendentals=0),
        name="mix_matrices",
    )(row_weight, col_weight)


def row_modes_kernel(place_ref, *refs):
    for table, source, target in zip(refs[0:2], refs[2:4], refs[4:6]):
        for g in range(source.shape[0] // GROUP):
            parts = []
            for half in range(2):
                first = g * GROUP + half * HALF_GROUP
                block = source[first : first + HALF_GROUP].reshape(-1, LANES)
                modes = jnp.dot(table[0], block, preferred_element_type=jnp.float32)
                parts.append(modes.reshape(-1, HALF_GROUP, LANES))
            at = slice(g * GROUP, (g + 1) * GROUP)
            target[:, at, :] = jnp.concatenate(parts, axis=1).astype(jnp.bfloat16)


def row_modes(place, tables, plane, mode_count, base, paired):
    channels, row_count, _ = plane.shape
    modes = 2 * mode_count if paired else mode_count
    groups = channels // STEP_CHANNELS
    shape = jax.ShapeDtypeStruct((modes, channels, LANES), jnp.bfloat16)
    block = pl.BlockSpec((modes, STEP_CHANNELS, LANES), lambda g, place: (0, g, 0))
    rows = modes * HALF_GROUP

    def table_at(which):
        return pl.BlockSpec(
            (1, rows, tables.shape[2]),
            lambda g, place: (place[2], 0 if paired else place[which], 0),
        )

    def plane_at(which):
        return pl.BlockSpec(
            (STEP_CHANNELS, row_count, LANES),
            lambda g, place: (g, 0, base + place[which] if paired else base),
        )

    return pl.pallas_call(
        row_modes_kernel,
        out_shape=(shape, shape),
        grid_spec=pltpu.PrefetchScalarGridSpec(
            num_scalar_prefetch=1,
            grid=(groups,),
            in_specs=[table_at(1), table_at(0), plane_at(1), plane_at(0)],
            out_specs=(block, block),
        ),
        compiler_params=pltpu.CompilerParams(vmem_limit_bytes=HEAD_VMEM_BYTES),
        cost_estimate=pl.CostEstimate(flops=0, bytes_accessed=0, transcendentals=0),
        name="row_modes",
    )(place, tables, tables, plane, plane)


def col_modes_kernel(table_ref, plane_ref, out_ref):
    block = plane_ref[...].reshape(-1, plane_ref.shape[2])
    out_ref[...] = lax.dot_general(
        table_ref[...], block, (((1,), (1,)), ((), ())), preferred_element_type=jnp.float32
    )


def col_modes(table, plane):
    channels, row_count, col_count = plane.shape
    modes = table.shape[0]
    return pl.pallas_call(
        col_modes_kernel,
        out_shape=jax.ShapeDtypeStruct((modes, channels * row_count), jnp.float32),
        grid=(channels // GROUP,),
        in_specs=[
            pl.BlockSpec((modes, col_count), lambda g: (0, 0)),
            pl.BlockSpec((GROUP, row_count, col_count), lambda g: (g, 0, 0)),
        ],
        out_specs=pl.BlockSpec((modes, GROUP * row_count), lambda g: (0, g)),
        compiler_params=pltpu.CompilerParams(vmem_limit_bytes=HEAD_VMEM_BYTES),
        cost_estimate=pl.CostEstimate(flops=0, bytes_accessed=0, transcendentals=0),
        name="col_modes",
    )(table, plane)


def finish_kernel(
    row_scale,
    paired,
    place_ref,
    modes_ref,
    more_ref,
    mix_ref,
    inverse_ref,
    local_ref,
    plane_ref,
    col_ref,
    up_ref,
    down_ref,
    down_bias_ref,
    order_ref,
    *rest,
):
    out_ref, mixed_ref, pre_ref, done_ref, rows_ref, wide_ref = rest[-6:]
    mode_rows, channels, _ = mixed_ref.shape
    row_count = plane_ref.shape[1]
    held = modes_ref.shape[0] // 2
    for which, source in enumerate((modes_ref,) if paired else (modes_ref, more_ref)):
        start = 0 if paired else place_ref[which] * held
        for k in range(held):
            pair = source[2 * k : 2 * k + 2].reshape(2 * channels, LANES)
            mixed = jnp.dot(mix_ref[start + k], pair, preferred_element_type=jnp.float32)
            mixed = (mixed * row_scale).astype(jnp.bfloat16)
            mixed_ref[pl.ds(2 * (start + k), 2)] = mixed.reshape(2, channels, LANES)
    for g in range(channels // GROUP):
        for h in range(row_count // GROUP):
            o, x = slice(g * GROUP, (g + 1) * GROUP), slice(h * GROUP, (h + 1) * GROUP)
            block = plane_ref[o, x, :].reshape(GROUP * GROUP, LANES)
            turned = jnp.dot(order_ref[...], block, preferred_element_type=jnp.float32)
            rows_ref[x, o, :] = turned.astype(jnp.bfloat16).reshape(GROUP, GROUP, LANES)
    for g in range(channels // GROUP):
        part = mixed_ref[:, g * GROUP : (g + 1) * GROUP, :].reshape(mode_rows * GROUP, LANES)
        rows = jnp.dot(inverse_ref[0], part, preferred_element_type=jnp.float32)
        pre_ref[:, g * GROUP : (g + 1) * GROUP, :] = rows.reshape(row_count, GROUP, LANES)
    cols = col_ref[...]

    def one_row(x):
        data = jnp.concatenate([rows_ref[x], cols], axis=0)
        local = jnp.dot(local_ref[x], data, preferred_element_type=jnp.float32)
        return (pre_ref[x] + local).astype(jnp.bfloat16)

    def gather(x, carry):
        at = pl.ds(pl.multiple_of(x * LANES, LANES), LANES)
        wide_ref[:channels, at] = one_row(x)
        return carry

    lax.fori_loop(0, row_count, gather, 0, unroll=32)
    wide_ref[channels:, :] = jnp.ones((BIAS_ROWS, wide_ref.shape[1]), jnp.bfloat16)
    bias = down_bias_ref[...]
    tiles = wide_ref.shape[1] // TILE

    def up(i):
        return jnp.dot(up_ref[...], wide_ref[:, i * TILE : (i + 1) * TILE], preferred_element_type=jnp.float32)

    def down(i, hidden):
        out = jnp.dot(down_ref[...], hidden, preferred_element_type=jnp.float32)
        for q in range(TILE // LANES):
            done_ref[i * (TILE // LANES) + q] = (out[:, q * LANES : (q + 1) * LANES] + bias).astype(jnp.bfloat16)

    waiting = up(0)
    hidden = None
    for i in range(tiles):
        following = up(i + 1) if i + 1 < tiles else None
        active = gelu(waiting).astype(jnp.bfloat16)
        if hidden is not None:
            down(i - 1, hidden)
        hidden, waiting = active, following
    down(tiles - 1, hidden)
    for g in range(channels // GROUP):
        for h in range(row_count // GROUP):
            o, x = slice(g * GROUP, (g + 1) * GROUP), slice(h * GROUP, (h + 1) * GROUP)
            block = done_ref[x, o, :].reshape(GROUP * GROUP, LANES)
            turned = jnp.dot(order_ref[...], block, preferred_element_type=jnp.float32)
            out_ref[o, x, :] = turned.astype(jnp.bfloat16).reshape(GROUP, GROUP, LANES)


def finish(place, base, which, modes, more, shared, plane, col_inverse, row_scale, out):
    paired = more is None
    more = modes if paired else more
    mode_rows = modes.shape[0] * (1 if paired else 2)

    def at(place):
        return base + place[which] if paired else base

    mix, inverse, local, up, down, down_bias, order = shared
    channels, row_count, col_count = plane.shape

    def whole(a):
        return pl.BlockSpec(a.shape, lambda i, place: (0,) * a.ndim)

    operands = [modes, more, mix, inverse, local, plane, col_inverse, up, down, down_bias, order]
    in_specs = [
        whole(modes),
        pl.BlockSpec(memory_space=pl.ANY) if paired else whole(more),
        whole(mix),
        pl.BlockSpec((1,) + inverse.shape[1:], lambda i, place: (place[2], 0, 0)),
        whole(local),
        pl.BlockSpec((channels, row_count, LANES), lambda i, place: (0, 0, at(place))),
        pl.BlockSpec((col_inverse.shape[0], LANES), lambda i, place: (0, at(place))),
        whole(up),
        whole(down),
        whole(down_bias),
        whole(order),
    ]
    aliases = {}
    if out is not None:
        operands.append(out)
        in_specs.append(pl.BlockSpec(memory_space=pl.ANY))
        aliases = {len(operands): 0}

    def kernel(*refs):
        finish_kernel(row_scale, paired, *refs)

    return pl.pallas_call(
        kernel,
        out_shape=jax.ShapeDtypeStruct((channels, row_count, col_count), jnp.bfloat16),
        grid_spec=pltpu.PrefetchScalarGridSpec(
            num_scalar_prefetch=1,
            grid=(1,),
            in_specs=in_specs,
            out_specs=pl.BlockSpec((channels, row_count, LANES), lambda i, place: (0, 0, at(place))),
            scratch_shapes=[
                pltpu.VMEM((mode_rows, channels, LANES), jnp.bfloat16),
                pltpu.VMEM((row_count, channels, LANES), jnp.float32),
                pltpu.VMEM((row_count, channels, LANES), jnp.bfloat16),
                pltpu.VMEM((row_count, channels, LANES), jnp.bfloat16),
                pltpu.VMEM((channels+BIAS_ROWS, row_count * LANES), jnp.bfloat16),
            ],
        ),
        input_output_aliases=aliases,
        compiler_params=pltpu.CompilerParams(vmem_limit_bytes=VMEM_BYTES),
        cost_estimate=pl.CostEstimate(flops=0, bytes_accessed=0, transcendentals=0),
        name="finish",
    )(place, *operands)


def add(a, b):
    return (a.astype(jnp.float32) + b.astype(jnp.float32)).astype(jnp.bfloat16)


NEAR = [(0, 1), (1, 0), (2, 3), (3, 2)]
FAR = [(0, 3), (3, 0), (1, 2), (2, 1)]


def sum_over_cols_axis(value):
    size = lax.axis_size("gy")
    if size & (size - 1):
        return lax.psum(value, "gy")
    step = 1
    while step < size:
        value = value + lax.ppermute(value, "gy", [(i, i ^ step) for i in range(size)])
        step *= 2
    return value


def body(
    plane_input, row_weight, col_weight, skip_weight, up_weight, up_bias, down_weight, down_bias
):
    channels, row_count, col_count = plane_input.shape
    mode_count = row_weight.shape[1]
    shares = lax.axis_size("gx")
    row_total = row_count * shares
    col_total = col_count * lax.axis_size("gy")
    row_scale = float(row_total * mode_count) ** (-0.5)
    col_scale = float(col_total * mode_count) ** (-0.5)
    share = lax.axis_index("gx")
    line = shares == 4
    inner = jnp.where((share == 1) | (share == 2), 1, 0) if line else jnp.zeros((), jnp.int32)
    place = jnp.stack([inner, 1 - inner, share]).astype(jnp.int32)
    blocks = col_count // LANES
    rounds = [(i, True) for i in range(0, blocks, 2)]
    tables = row_tables(mode_count, shares, row_count)

    partial = [row_modes(place, tables, plane_input, mode_count, *r) for r in rounds]
    if line:
        near = [lax.ppermute(send, "gx", NEAR) for send, _ in partial]
        half = [add(keep, got) for (_, keep), got in zip(partial, near)]
        far = [lax.ppermute(value, "gx", FAR) for value in half]
    else:
        own = [lax.psum(keep.astype(jnp.float32), "gx").astype(jnp.bfloat16) for _, keep in partial]
        other = [lax.psum(send.astype(jnp.float32), "gx").astype(jnp.bfloat16) for send, _ in partial]

    row_mix, col_mix = mix_matrices(row_weight, col_weight)
    col_offset = lax.axis_index("gy") * col_count
    col_partial = col_modes(forward_table(mode_count, col_total, col_offset, col_count), plane_input)
    col_spectrum = sum_over_cols_axis(col_partial)
    if line:
        mine, col_spectrum = lax.optimization_barrier((add(half[0], far[0]), col_spectrum))
        theirs = lax.ppermute(mine, "gx", NEAR)
    col_spectrum = col_spectrum.astype(jnp.bfloat16).reshape(mode_count, 2 * channels, row_count)
    col_mixed = jnp.einsum(
        "koc,kcx->kox", col_mix, col_spectrum, preferred_element_type=jnp.float32
    )
    col_mixed = (col_mixed * col_scale).astype(jnp.bfloat16)
    col_mixed = col_mixed.reshape(2 * mode_count, channels, row_count).transpose(2, 1, 0)
    skip = jnp.broadcast_to(skip_weight.T[None], (row_count, channels, channels))
    local = jnp.concatenate([skip, col_mixed], axis=2)
    col_inverse = inverse_table(mode_count, col_total, col_offset, col_count)
    high = lax.reduce_precision(up_bias, 8, 7)
    middle = lax.reduce_precision(up_bias - high, 8, 7)
    low = up_bias - high - middle
    bias_part = jnp.pad(jnp.stack([high, middle, low], axis=1), ((0, 0), (0, BIAS_ROWS - 3)))
    bias_part = bias_part.astype(jnp.bfloat16)
    up = jnp.concatenate([up_weight.T, bias_part], axis=1)
    order = np.zeros((GROUP, GROUP, GROUP, GROUP), np.float32)
    for a in range(GROUP):
        for b in range(GROUP):
            order[a, b, b, a] = 1.0
    order = jnp.asarray(order.reshape(GROUP * GROUP, GROUP * GROUP), jnp.bfloat16)
    shared = (
        row_mix,
        row_inverse_tables(mode_count, shares, row_count),
        local,
        up,
        down_weight.T,
        jnp.broadcast_to(down_bias[:, None], (channels, LANES)),
        order,
    )
    out = None
    common = (shared, plane_input, col_inverse, row_scale)
    if line:
        for i, (base, paired) in enumerate(rounds):
            out = finish(place, base, 0, mine, None, *common, out)
            if i + 1 < len(rounds):
                summed, out = lax.optimization_barrier((half[i + 1], out))
                following = add(summed, far[i + 1])
                sent = lax.ppermute(following, "gx", NEAR)
                out = finish(place, base, 1, theirs, None, *common, out)
                mine, theirs = following, sent
            else:
                out = finish(place, base, 1, theirs, None, *common, out)
    else:
        for (base, paired), mine, theirs in zip(rounds, own, other):
            out = finish(place, base, 0, mine, None, *common, out)
            out = finish(place, base, 1, theirs, None, *common, out)
    return out


def solution(mesh):
    placed = (P(None, ("grp", "gx"), "gy"), P(), P(), P(), P(), P(), P(), P())
    return jax.shard_map(
        body, mesh=mesh, in_specs=placed, out_specs=P(None, ("grp", "gx"), "gy"), check_vma=False
    )
```

```python
import math

import jax
import jax.numpy as jnp
import numpy as np
from jax import lax
from jax.experimental import pallas as pl
from jax.experimental.pallas import tpu as pltpu
from jax.sharding import PartitionSpec as P

LANES = 128
GROUP = 16
HALF_GROUP = 8
BIAS_ROWS = 16
STEP_CHANNELS = 32
TILE = 512
VMEM_BYTES = 24 * 1024 * 1024
HEAD_VMEM_BYTES = 63 * 1024 * 1024

TAIL = 0.4
COEFFS = (0.15957266, 0.16051476, 0.12055834, 0.14408696, -0.08478078)
EXP_SCALE = -0.5 * math.log2(math.e)


def gelu(v):
    t = jnp.abs(v)
    s = 1.0 / (1.0 + TAIL * t)
    poly = COEFFS[-1]
    for c in COEFFS[-2::-1]:
        poly = poly * s + c
    return jnp.maximum(v, 0.0) - jnp.exp2(t * t * EXP_SCALE) * (poly * s) * t


def row_tables(mode_count, shares, row_count):
    period = shares * row_count
    phases = np.arange(mode_count)[:, None] * np.arange(period)[None, :] % period
    angles = phases.astype(np.float64) * (2.0 * math.pi / period)
    table = np.stack([np.cos(angles), -np.sin(angles)], axis=1).reshape(2 * mode_count, shares, row_count)
    eye = np.eye(HALF_GROUP)
    whole = np.einsum("jsx,cd->sjcdx", table, eye)
    return jnp.asarray(
        whole.reshape(shares, 2 * mode_count * HALF_GROUP, HALF_GROUP * row_count), jnp.bfloat16
    )


def row_inverse_tables(mode_count, shares, row_count):
    period = shares * row_count
    phases = np.arange(period)[:, None] * np.arange(mode_count)[None, :] % period
    angles = phases.astype(np.float64) * (2.0 * math.pi / period)
    factors = np.where(np.arange(mode_count) == 0, 1.0, 2.0)
    table = np.stack([factors * np.cos(angles), -factors * np.sin(angles)], axis=2)
    table = table.reshape(shares, row_count, 2 * mode_count)
    whole = np.einsum("sxj,cd->sxcjd", table, np.eye(GROUP))
    return jnp.asarray(
        whole.reshape(shares, row_count * GROUP, 2 * mode_count * GROUP), jnp.bfloat16
    )


def forward_table(mode_count, period, offset, number):
    wave_index = jnp.arange(mode_count, dtype=jnp.int32)
    cell_index = offset + jnp.arange(number, dtype=jnp.int32)
    phases = wave_index[:, None] * cell_index[None, :] % period
    angles = phases.astype(jnp.float32) * (2.0 * math.pi / period)
    both = jnp.stack([jnp.cos(angles), -jnp.sin(angles)], axis=1)
    return both.reshape(2 * mode_count, number).astype(jnp.bfloat16)


def inverse_table(mode_count, period, offset, number):
    wave_index = jnp.arange(mode_count, dtype=jnp.int32)
    cell_index = offset + jnp.arange(number, dtype=jnp.int32)
    phases = wave_index[:, None] * cell_index[None, :] % period
    angles = phases.astype(jnp.float32) * (2.0 * math.pi / period)
    factors = jnp.where(wave_index == 0, 1.0, 2.0).astype(jnp.float32)[:, None]
    both = jnp.stack([factors * jnp.cos(angles), -factors * jnp.sin(angles)], axis=1)
    return both.reshape(2 * mode_count, number).astype(jnp.bfloat16)


def mix_kernel(row_ref, col_ref, row_out_ref, col_out_ref):
    for source, target in ((row_ref, row_out_ref), (col_ref, col_out_ref)):
        for k in range(source.shape[1]):
            real = source[0, k].astype(jnp.float32).T
            imag = source[1, k].astype(jnp.float32).T
            upper = jnp.concatenate([real, -imag], axis=1)
            lower = jnp.concatenate([imag, real], axis=1)
            target[k] = jnp.concatenate([upper, lower], axis=0).astype(jnp.bfloat16)


def mix_matrices(row_weight, col_weight):
    _, modes, channels, _ = row_weight.shape
    shape = jax.ShapeDtypeStruct((modes, 2 * channels, 2 * channels), jnp.bfloat16)
    return pl.pallas_call(
        mix_kernel,
        out_shape=(shape, shape),
        compiler_params=pltpu.CompilerParams(vmem_limit_bytes=VMEM_BYTES),
        cost_estimate=pl.CostEstimate(flops=0, bytes_accessed=0, transcendentals=0),
        name="mix_matrices",
    )(row_weight, col_weight)


def row_modes_kernel(place_ref, table, *refs):
    for source, target in zip(refs[:2], refs[2:]):
        for g in range(source.shape[0] // GROUP):
            parts = []
            for half in range(2):
                first = g * GROUP + half * HALF_GROUP
                block = source[first : first + HALF_GROUP].reshape(-1, LANES)
                modes = jnp.dot(table[0], block, preferred_element_type=jnp.float32)
                parts.append(modes.reshape(-1, HALF_GROUP, LANES))
            at = slice(g * GROUP, (g + 1) * GROUP)
            target[:, at, :] = jnp.concatenate(parts, axis=1).astype(jnp.bfloat16)


def row_modes(place, tables, plane, mode_count, base):
    channels, row_count, _ = plane.shape
    modes = 2 * mode_count
    groups = channels // STEP_CHANNELS
    shape = jax.ShapeDtypeStruct((modes, channels, LANES), jnp.bfloat16)
    block = pl.BlockSpec((modes, STEP_CHANNELS, LANES), lambda g, place: (0, g, 0))
    rows = modes * HALF_GROUP

    table_at = pl.BlockSpec((1, rows, tables.shape[2]), lambda g, place: (place[2], 0, 0))

    def plane_at(which):
        return pl.BlockSpec(
            (STEP_CHANNELS, row_count, LANES),
            lambda g, place: (g, 0, base + place[which]),
        )

    return pl.pallas_call(
        row_modes_kernel,
        out_shape=(shape, shape),
        grid_spec=pltpu.PrefetchScalarGridSpec(
            num_scalar_prefetch=1,
            grid=(groups,),
            in_specs=[table_at, plane_at(1), plane_at(0)],
            out_specs=(block, block),
        ),
        compiler_params=pltpu.CompilerParams(vmem_limit_bytes=HEAD_VMEM_BYTES),
        cost_estimate=pl.CostEstimate(flops=0, bytes_accessed=0, transcendentals=0),
        name="row_modes",
    )(place, tables, plane, plane)


def col_modes_kernel(table_ref, plane_ref, out_ref):
    block = plane_ref[...].reshape(-1, plane_ref.shape[2])
    out_ref[...] = lax.dot_general(
        table_ref[...], block, (((1,), (1,)), ((), ())), preferred_element_type=jnp.float32
    )


def col_modes(table, plane):
    channels, row_count, col_count = plane.shape
    modes = table.shape[0]
    return pl.pallas_call(
        col_modes_kernel,
        out_shape=jax.ShapeDtypeStruct((modes, channels * row_count), jnp.float32),
        grid=(channels // GROUP,),
        in_specs=[
            pl.BlockSpec((modes, col_count), lambda g: (0, 0)),
            pl.BlockSpec((GROUP, row_count, col_count), lambda g: (g, 0, 0)),
        ],
        out_specs=pl.BlockSpec((modes, GROUP * row_count), lambda g: (0, g)),
        compiler_params=pltpu.CompilerParams(vmem_limit_bytes=HEAD_VMEM_BYTES),
        cost_estimate=pl.CostEstimate(flops=0, bytes_accessed=0, transcendentals=0),
        name="col_modes",
    )(table, plane)


def finish_kernel(
    row_scale,
    single,
    place_ref,
    modes_ref,
    more_ref,
    mix_ref,
    inverse_ref,
    local_ref,
    plane_ref,
    col_ref,
    up_ref,
    down_ref,
    down_bias_ref,
    order_ref,
    *rest,
):
    out_ref, mixed_ref, pre_ref, done_ref, rows_ref, wide_ref = rest[-6:]
    mode_rows, channels, _ = mixed_ref.shape
    row_count = plane_ref.shape[1]

    def mix(source):
        for k in range(mode_rows // 2):
            pair = source[2 * k : 2 * k + 2].reshape(2 * channels, LANES)
            mixed = jnp.dot(mix_ref[k], pair, preferred_element_type=jnp.float32)
            mixed = (mixed * row_scale).astype(jnp.bfloat16)
            mixed_ref[2 * k : 2 * k + 2] = mixed.reshape(2, channels, LANES)

    if single:
        mix(modes_ref)
    else:
        pl.when(pl.program_id(0) == 0)(lambda: mix(modes_ref))
        pl.when(pl.program_id(0) == 1)(lambda: mix(more_ref))
    for g in range(channels // GROUP):
        for h in range(row_count // GROUP):
            o, x = slice(g * GROUP, (g + 1) * GROUP), slice(h * GROUP, (h + 1) * GROUP)
            block = plane_ref[o, x, :].reshape(GROUP * GROUP, LANES)
            turned = jnp.dot(order_ref[...], block, preferred_element_type=jnp.float32)
            rows_ref[x, o, :] = turned.astype(jnp.bfloat16).reshape(GROUP, GROUP, LANES)
    for g in range(channels // GROUP):
        part = mixed_ref[:, g * GROUP : (g + 1) * GROUP, :].reshape(mode_rows * GROUP, LANES)
        rows = jnp.dot(inverse_ref[0], part, preferred_element_type=jnp.float32)
        pre_ref[:, g * GROUP : (g + 1) * GROUP, :] = rows.reshape(row_count, GROUP, LANES)
    cols = col_ref[...]

    def one_row(x):
        data = jnp.concatenate([rows_ref[x], cols], axis=0)
        local = jnp.dot(local_ref[x], data, preferred_element_type=jnp.float32)
        return (pre_ref[x] + local).astype(jnp.bfloat16)

    def gather(x, carry):
        at = pl.ds(pl.multiple_of(x * LANES, LANES), LANES)
        wide_ref[:channels, at] = one_row(x)
        return carry

    lax.fori_loop(0, row_count, gather, 0, unroll=32)
    wide_ref[channels:, :] = jnp.ones((BIAS_ROWS, wide_ref.shape[1]), jnp.bfloat16)
    bias = down_bias_ref[...]
    tiles = wide_ref.shape[1] // TILE

    def up(i):
        return jnp.dot(up_ref[...], wide_ref[:, i * TILE : (i + 1) * TILE], preferred_element_type=jnp.float32)

    def down(i, hidden):
        out = jnp.dot(down_ref[...], hidden, preferred_element_type=jnp.float32)
        for q in range(TILE // LANES):
            done_ref[i * (TILE // LANES) + q] = (out[:, q * LANES : (q + 1) * LANES] + bias).astype(jnp.bfloat16)

    waiting = up(0)
    hidden = None
    for i in range(tiles):
        following = up(i + 1) if i + 1 < tiles else None
        active = gelu(waiting).astype(jnp.bfloat16)
        if hidden is not None:
            down(i - 1, hidden)
        hidden, waiting = active, following
    down(tiles - 1, hidden)
    for g in range(channels // GROUP):
        for h in range(row_count // GROUP):
            o, x = slice(g * GROUP, (g + 1) * GROUP), slice(h * GROUP, (h + 1) * GROUP)
            block = done_ref[x, o, :].reshape(GROUP * GROUP, LANES)
            turned = jnp.dot(order_ref[...], block, preferred_element_type=jnp.float32)
            out_ref[o, x, :] = turned.astype(jnp.bfloat16).reshape(GROUP, GROUP, LANES)


def finish(place, at, modes, shared, plane, col_inverse, row_scale, out):
    mix, inverse, local, up, down, down_bias, order = shared
    single = len(modes) == 1
    modes, more = modes[0], modes[-1]
    mode_rows = modes.shape[0]

    def column(i, place):
        (base, which), (last_base, last_which) = at[0], at[-1]
        first = base + place[which]
        return first if single else jnp.where(i == 0, first, last_base + place[last_which])

    channels, row_count, col_count = plane.shape

    def whole(a):
        return pl.BlockSpec(a.shape, lambda i, place: (0,) * a.ndim)

    operands = [modes, more, mix, inverse, local, plane, col_inverse, up, down, down_bias, order]
    in_specs = [
        whole(modes),
        pl.BlockSpec(memory_space=pl.ANY) if single else whole(more),
        whole(mix),
        pl.BlockSpec((1,) + inverse.shape[1:], lambda i, place: (place[2], 0, 0)),
        whole(local),
        pl.BlockSpec((channels, row_count, LANES), lambda i, place: (0, 0, column(i, place))),
        pl.BlockSpec((col_inverse.shape[0], LANES), lambda i, place: (0, column(i, place))),
        whole(up),
        whole(down),
        whole(down_bias),
        whole(order),
    ]
    aliases = {}
    if out is not None:
        operands.append(out)
        in_specs.append(pl.BlockSpec(memory_space=pl.ANY))
        aliases = {len(operands): 0}

    def kernel(*refs):
        finish_kernel(row_scale, single, *refs)

    return pl.pallas_call(
        kernel,
        out_shape=jax.ShapeDtypeStruct((channels, row_count, col_count), jnp.bfloat16),
        grid_spec=pltpu.PrefetchScalarGridSpec(
            num_scalar_prefetch=1,
            grid=(1 if single else 2,),
            in_specs=in_specs,
            out_specs=pl.BlockSpec((channels, row_count, LANES), lambda i, place: (0, 0, column(i, place))),
            scratch_shapes=[
                pltpu.VMEM((mode_rows, channels, LANES), jnp.bfloat16),
                pltpu.VMEM((row_count, channels, LANES), jnp.float32),
                pltpu.VMEM((row_count, channels, LANES), jnp.bfloat16),
                pltpu.VMEM((row_count, channels, LANES), jnp.bfloat16),
                pltpu.VMEM((channels+BIAS_ROWS, row_count * LANES), jnp.bfloat16),
            ],
        ),
        input_output_aliases=aliases,
        compiler_params=pltpu.CompilerParams(vmem_limit_bytes=VMEM_BYTES),
        cost_estimate=pl.CostEstimate(flops=0, bytes_accessed=0, transcendentals=0),
        name="finish",
    )(place, *operands)


def add(a, b):
    return (a.astype(jnp.float32) + b.astype(jnp.float32)).astype(jnp.bfloat16)


NEAR = [(0, 1), (1, 0), (2, 3), (3, 2)]
FAR = [(0, 3), (3, 0), (1, 2), (2, 1)]


def sum_over_cols_axis(value):
    size = lax.axis_size("gy")
    if size & (size - 1):
        return lax.psum(value, "gy")
    step = 1
    while step < size:
        value = value + lax.ppermute(value, "gy", [(i, i ^ step) for i in range(size)])
        step *= 2
    return value


def body(
    plane_input, row_weight, col_weight, skip_weight, up_weight, up_bias, down_weight, down_bias
):
    channels, row_count, col_count = plane_input.shape
    mode_count = row_weight.shape[1]
    shares = lax.axis_size("gx")
    row_total = row_count * shares
    col_total = col_count * lax.axis_size("gy")
    row_scale = float(row_total * mode_count) ** (-0.5)
    col_scale = float(col_total * mode_count) ** (-0.5)
    share = lax.axis_index("gx")
    line = shares == 4
    inner = jnp.where((share == 1) | (share == 2), 1, 0) if line else jnp.zeros((), jnp.int32)
    place = jnp.stack([inner, 1 - inner, share]).astype(jnp.int32)
    blocks = col_count // LANES
    rounds = list(range(0, blocks, 2))
    tables = row_tables(mode_count, shares, row_count)

    partial = [row_modes(place, tables, plane_input, mode_count, base) for base in rounds]
    if line:
        near = [lax.ppermute(send, "gx", NEAR) for send, _ in partial]
        half = [add(keep, got) for (_, keep), got in zip(partial, near)]
    else:
        own = [lax.psum(keep.astype(jnp.float32), "gx").astype(jnp.bfloat16) for _, keep in partial]
        other = [lax.psum(send.astype(jnp.float32), "gx").astype(jnp.bfloat16) for send, _ in partial]

    row_mix, col_mix = mix_matrices(row_weight, col_weight)
    col_offset = lax.axis_index("gy") * col_count
    col_partial = col_modes(forward_table(mode_count, col_total, col_offset, col_count), plane_input)
    col_spectrum = sum_over_cols_axis(col_partial)
    if line:
        half[1], col_spectrum = lax.optimization_barrier((half[1], col_spectrum))
        far = [lax.ppermute(value, "gx", FAR) for value in half]
    col_spectrum = col_spectrum.astype(jnp.bfloat16).reshape(mode_count, 2 * channels, row_count)
    col_mixed = jnp.einsum(
        "koc,kcx->kox", col_mix, col_spectrum, preferred_element_type=jnp.float32
    )
    col_mixed = (col_mixed * col_scale).astype(jnp.bfloat16)
    col_mixed = col_mixed.reshape(2 * mode_count, channels, row_count).transpose(2, 1, 0)
    skip = jnp.broadcast_to(skip_weight.T[None], (row_count, channels, channels))
    local = jnp.concatenate([skip, col_mixed], axis=2)
    col_inverse = inverse_table(mode_count, col_total, col_offset, col_count)
    high = lax.reduce_precision(up_bias, 8, 7)
    middle = lax.reduce_precision(up_bias - high, 8, 7)
    low = up_bias - high - middle
    bias_part = jnp.pad(jnp.stack([high, middle, low], axis=1), ((0, 0), (0, BIAS_ROWS - 3)))
    bias_part = bias_part.astype(jnp.bfloat16)
    up = jnp.concatenate([up_weight.T, bias_part], axis=1)
    order = np.zeros((GROUP, GROUP, GROUP, GROUP), np.float32)
    for a in range(GROUP):
        for b in range(GROUP):
            order[a, b, b, a] = 1.0
    order = jnp.asarray(order.reshape(GROUP * GROUP, GROUP * GROUP), jnp.bfloat16)
    shared = (
        row_mix,
        row_inverse_tables(mode_count, shares, row_count),
        local,
        up,
        down_weight.T,
        jnp.broadcast_to(down_bias[:, None], (channels, LANES)),
        order,
    )
    out = None
    common = (shared, plane_input, col_inverse, row_scale)
    if line:
        waiting = []
        for i, base in enumerate(rounds):
            summed = half[i]
            if out is not None:
                summed, out = lax.optimization_barrier((summed, out))
            mine = add(summed, far[i])
            theirs = lax.ppermute(mine, "gx", NEAR)
            ready = waiting + [((base, 0), mine)]
            out = finish(place, [w[0] for w in ready], [w[1] for w in ready], *common, out)
            waiting = [((base, 1), theirs)]
        out = finish(place, [waiting[0][0]], [waiting[0][1]], *common, out)
    else:
        for base, mine, theirs in zip(rounds, own, other):
            out = finish(place, [(base, 0), (base, 1)], [mine, theirs], *common, out)
    return out


def solution(mesh):
    placed = (P(None, ("grp", "gx"), "gy"), P(), P(), P(), P(), P(), P(), P())
    return jax.shard_map(
        body, mesh=mesh, in_specs=placed, out_specs=P(None, ("grp", "gx"), "gy"), check_vma=False
    )
```

```python
import math

import jax
import jax.numpy as jnp
import numpy as np
from jax import lax
from jax.experimental import pallas as pl
from jax.experimental.pallas import tpu as pltpu
from jax.sharding import PartitionSpec as P

LANES = 128
GROUP = 16
HALF_GROUP = 8
BIAS_ROWS = 16
STEP_CHANNELS = 32
TILE = 512
VMEM_BYTES = 24 * 1024 * 1024
HEAD_VMEM_BYTES = 63 * 1024 * 1024

TAIL = 0.4
COEFFS = (0.15957266, 0.16051476, 0.12055834, 0.14408696, -0.08478078)
EXP_SCALE = -0.5 * math.log2(math.e)


def gelu(v):
    t = jnp.abs(v)
    s = 1.0 / (1.0 + TAIL * t)
    poly = COEFFS[-1]
    for c in COEFFS[-2::-1]:
        poly = poly * s + c
    return jnp.maximum(v, 0.0) - jnp.exp2(t * t * EXP_SCALE) * (poly * s) * t


def row_tables(mode_count, shares, row_count):
    period = shares * row_count
    phases = np.arange(mode_count)[:, None] * np.arange(period)[None, :] % period
    angles = phases.astype(np.float64) * (2.0 * math.pi / period)
    table = np.stack([np.cos(angles), -np.sin(angles)], axis=1).reshape(2 * mode_count, shares, row_count)
    table = np.concatenate([table[:1], table[2:], table[1:2]], axis=0)
    eye = np.eye(HALF_GROUP)
    whole = np.einsum("jsx,cd->sjcdx", table, eye)
    return jnp.asarray(
        whole.reshape(shares, 2 * mode_count * HALF_GROUP, HALF_GROUP * row_count), jnp.bfloat16
    )


def row_inverse_tables(mode_count, shares, row_count):
    period = shares * row_count
    phases = np.arange(period)[:, None] * np.arange(mode_count)[None, :] % period
    angles = phases.astype(np.float64) * (2.0 * math.pi / period)
    factors = np.where(np.arange(mode_count) == 0, 1.0, 2.0)
    table = np.stack([factors * np.cos(angles), -factors * np.sin(angles)], axis=2)
    table = table.reshape(shares, row_count, 2 * mode_count)
    whole = np.einsum("sxj,cd->sxcjd", table, np.eye(GROUP))
    return jnp.asarray(
        whole.reshape(shares, row_count * GROUP, 2 * mode_count * GROUP), jnp.bfloat16
    )


def forward_table(mode_count, period, offset, number):
    wave_index = jnp.arange(mode_count, dtype=jnp.int32)
    cell_index = offset + jnp.arange(number, dtype=jnp.int32)
    phases = wave_index[:, None] * cell_index[None, :] % period
    angles = phases.astype(jnp.float32) * (2.0 * math.pi / period)
    both = jnp.stack([jnp.cos(angles), -jnp.sin(angles)], axis=1)
    return both.reshape(2 * mode_count, number).astype(jnp.bfloat16)


def inverse_table(mode_count, period, offset, number):
    wave_index = jnp.arange(mode_count, dtype=jnp.int32)
    cell_index = offset + jnp.arange(number, dtype=jnp.int32)
    phases = wave_index[:, None] * cell_index[None, :] % period
    angles = phases.astype(jnp.float32) * (2.0 * math.pi / period)
    factors = jnp.where(wave_index == 0, 1.0, 2.0).astype(jnp.float32)[:, None]
    both = jnp.stack([factors * jnp.cos(angles), -factors * jnp.sin(angles)], axis=1)
    return both.reshape(2 * mode_count, number).astype(jnp.bfloat16)


def mix_kernel(row_ref, col_ref, row_out_ref, col_out_ref):
    for source, target in ((row_ref, row_out_ref), (col_ref, col_out_ref)):
        for k in range(source.shape[1]):
            real = source[0, k].astype(jnp.float32).T
            imag = source[1, k].astype(jnp.float32).T
            upper = jnp.concatenate([real, -imag], axis=1)
            lower = jnp.concatenate([imag, real], axis=1)
            target[k] = jnp.concatenate([upper, lower], axis=0).astype(jnp.bfloat16)


def mix_matrices(row_weight, col_weight):
    _, modes, channels, _ = row_weight.shape
    shape = jax.ShapeDtypeStruct((modes, 2 * channels, 2 * channels), jnp.bfloat16)
    return pl.pallas_call(
        mix_kernel,
        out_shape=(shape, shape),
        compiler_params=pltpu.CompilerParams(vmem_limit_bytes=VMEM_BYTES),
        cost_estimate=pl.CostEstimate(flops=0, bytes_accessed=0, transcendentals=0),
        name="mix_matrices",
    )(row_weight, col_weight)


def row_modes_kernel(place_ref, table, *refs):
    for source, target in zip(refs[:2], refs[2:]):
        for g in range(source.shape[0] // GROUP):
            parts = []
            for half in range(2):
                first = g * GROUP + half * HALF_GROUP
                block = source[first : first + HALF_GROUP].reshape(-1, LANES)
                modes = jnp.dot(table[0], block, preferred_element_type=jnp.float32)
                parts.append(modes.reshape(-1, HALF_GROUP, LANES))
            at = slice(g * GROUP, (g + 1) * GROUP)
            target[:, at, :] = jnp.concatenate(parts, axis=1)[: target.shape[0]].astype(jnp.bfloat16)


def row_modes(place, tables, plane, mode_count, base):
    channels, row_count, _ = plane.shape
    modes = 2 * mode_count - 1
    groups = channels // STEP_CHANNELS
    shape = jax.ShapeDtypeStruct((modes, channels, LANES), jnp.bfloat16)
    block = pl.BlockSpec((modes, STEP_CHANNELS, LANES), lambda g, place: (0, g, 0))
    rows = tables.shape[1]

    table_at = pl.BlockSpec((1, rows, tables.shape[2]), lambda g, place: (place[2], 0, 0))

    def plane_at(which):
        return pl.BlockSpec(
            (STEP_CHANNELS, row_count, LANES),
            lambda g, place: (g, 0, base + place[which]),
        )

    return pl.pallas_call(
        row_modes_kernel,
        out_shape=(shape, shape),
        grid_spec=pltpu.PrefetchScalarGridSpec(
            num_scalar_prefetch=1,
            grid=(groups,),
            in_specs=[table_at, plane_at(1), plane_at(0)],
            out_specs=(block, block),
        ),
        compiler_params=pltpu.CompilerParams(vmem_limit_bytes=HEAD_VMEM_BYTES),
        cost_estimate=pl.CostEstimate(flops=0, bytes_accessed=0, transcendentals=0),
        name="row_modes",
    )(place, tables, plane, plane)


def col_modes_kernel(table_ref, plane_ref, out_ref):
    block = plane_ref[...].reshape(-1, plane_ref.shape[2])
    out_ref[...] = lax.dot_general(
        table_ref[...], block, (((1,), (1,)), ((), ())), preferred_element_type=jnp.float32
    )


def col_modes(table, plane):
    channels, row_count, col_count = plane.shape
    modes = table.shape[0]
    return pl.pallas_call(
        col_modes_kernel,
        out_shape=jax.ShapeDtypeStruct((modes, channels * row_count), jnp.float32),
        grid=(channels // GROUP,),
        in_specs=[
            pl.BlockSpec((modes, col_count), lambda g: (0, 0)),
            pl.BlockSpec((GROUP, row_count, col_count), lambda g: (g, 0, 0)),
        ],
        out_specs=pl.BlockSpec((modes, GROUP * row_count), lambda g: (0, g)),
        compiler_params=pltpu.CompilerParams(vmem_limit_bytes=HEAD_VMEM_BYTES),
        cost_estimate=pl.CostEstimate(flops=0, bytes_accessed=0, transcendentals=0),
        name="col_modes",
    )(table, plane)


def finish_kernel(
    row_scale,
    single,
    place_ref,
    modes_ref,
    more_ref,
    mix_ref,
    inverse_ref,
    local_ref,
    plane_ref,
    col_ref,
    up_ref,
    down_ref,
    down_bias_ref,
    order_ref,
    *rest,
):
    out_ref, mixed_ref, pre_ref, done_ref, rows_ref, wide_ref = rest[-6:]
    mode_rows, channels, _ = mixed_ref.shape
    row_count = plane_ref.shape[1]

    def mix(source):
        for k in range(mode_rows // 2):
            if k:
                pair = source[2 * k - 1 : 2 * k + 1].reshape(2 * channels, LANES)
                mixed = jnp.dot(mix_ref[k], pair, preferred_element_type=jnp.float32)
            else:
                mixed = jnp.dot(mix_ref[0, :, :channels], source[0], preferred_element_type=jnp.float32)
            mixed = (mixed * row_scale).astype(jnp.bfloat16)
            mixed_ref[2 * k : 2 * k + 2] = mixed.reshape(2, channels, LANES)

    if single:
        mix(modes_ref)
    else:
        pl.when(pl.program_id(0) == 0)(lambda: mix(modes_ref))
        pl.when(pl.program_id(0) == 1)(lambda: mix(more_ref))
    for g in range(channels // GROUP):
        for h in range(row_count // GROUP):
            o, x = slice(g * GROUP, (g + 1) * GROUP), slice(h * GROUP, (h + 1) * GROUP)
            block = plane_ref[o, x, :].reshape(GROUP * GROUP, LANES)
            turned = jnp.dot(order_ref[...], block, preferred_element_type=jnp.float32)
            rows_ref[x, o, :] = turned.astype(jnp.bfloat16).reshape(GROUP, GROUP, LANES)
    for g in range(channels // GROUP):
        part = mixed_ref[:, g * GROUP : (g + 1) * GROUP, :].reshape(mode_rows * GROUP, LANES)
        rows = jnp.dot(inverse_ref[0], part, preferred_element_type=jnp.float32)
        pre_ref[:, g * GROUP : (g + 1) * GROUP, :] = rows.reshape(row_count, GROUP, LANES)
    cols = col_ref[...]

    def one_row(x):
        data = jnp.concatenate([rows_ref[x], cols], axis=0)
        local = jnp.dot(local_ref[x], data, preferred_element_type=jnp.float32)
        return (pre_ref[x] + local).astype(jnp.bfloat16)

    def gather(x, carry):
        at = pl.ds(pl.multiple_of(x * LANES, LANES), LANES)
        wide_ref[:channels, at] = one_row(x)
        return carry

    lax.fori_loop(0, row_count, gather, 0, unroll=32)
    wide_ref[channels:, :] = jnp.ones((BIAS_ROWS, wide_ref.shape[1]), jnp.bfloat16)
    bias = down_bias_ref[...]
    tiles = wide_ref.shape[1] // TILE

    def up(i):
        return jnp.dot(up_ref[...], wide_ref[:, i * TILE : (i + 1) * TILE], preferred_element_type=jnp.float32)

    def down(i, hidden):
        out = jnp.dot(down_ref[...], hidden, preferred_element_type=jnp.float32)
        for q in range(TILE // LANES):
            done_ref[i * (TILE // LANES) + q] = (out[:, q * LANES : (q + 1) * LANES] + bias).astype(jnp.bfloat16)

    waiting = up(0)
    hidden = None
    for i in range(tiles):
        following = up(i + 1) if i + 1 < tiles else None
        active = gelu(waiting).astype(jnp.bfloat16)
        if hidden is not None:
            down(i - 1, hidden)
        hidden, waiting = active, following
    down(tiles - 1, hidden)
    for g in range(channels // GROUP):
        for h in range(row_count // GROUP):
            o, x = slice(g * GROUP, (g + 1) * GROUP), slice(h * GROUP, (h + 1) * GROUP)
            block = done_ref[x, o, :].reshape(GROUP * GROUP, LANES)
            turned = jnp.dot(order_ref[...], block, preferred_element_type=jnp.float32)
            out_ref[o, x, :] = turned.astype(jnp.bfloat16).reshape(GROUP, GROUP, LANES)


def finish(place, at, modes, shared, plane, col_inverse, row_scale, out):
    mix, inverse, local, up, down, down_bias, order = shared
    single = len(modes) == 1
    modes, more = modes[0], modes[-1]
    mode_rows = modes.shape[0] + 1

    def column(i, place):
        (base, which), (last_base, last_which) = at[0], at[-1]
        first = base + place[which]
        return first if single else jnp.where(i == 0, first, last_base + place[last_which])

    channels, row_count, col_count = plane.shape

    def whole(a):
        return pl.BlockSpec(a.shape, lambda i, place: (0,) * a.ndim)

    operands = [modes, more, mix, inverse, local, plane, col_inverse, up, down, down_bias, order]
    in_specs = [
        whole(modes),
        pl.BlockSpec(memory_space=pl.ANY) if single else whole(more),
        whole(mix),
        pl.BlockSpec((1,) + inverse.shape[1:], lambda i, place: (place[2], 0, 0)),
        whole(local),
        pl.BlockSpec((channels, row_count, LANES), lambda i, place: (0, 0, column(i, place))),
        pl.BlockSpec((col_inverse.shape[0], LANES), lambda i, place: (0, column(i, place))),
        whole(up),
        whole(down),
        whole(down_bias),
        whole(order),
    ]
    aliases = {}
    if out is not None:
        operands.append(out)
        in_specs.append(pl.BlockSpec(memory_space=pl.ANY))
        aliases = {len(operands): 0}

    def kernel(*refs):
        finish_kernel(row_scale, single, *refs)

    return pl.pallas_call(
        kernel,
        out_shape=jax.ShapeDtypeStruct((channels, row_count, col_count), jnp.bfloat16),
        grid_spec=pltpu.PrefetchScalarGridSpec(
            num_scalar_prefetch=1,
            grid=(1 if single else 2,),
            in_specs=in_specs,
            out_specs=pl.BlockSpec((channels, row_count, LANES), lambda i, place: (0, 0, column(i, place))),
            scratch_shapes=[
                pltpu.VMEM((mode_rows, channels, LANES), jnp.bfloat16),
                pltpu.VMEM((row_count, channels, LANES), jnp.float32),
                pltpu.VMEM((row_count, channels, LANES), jnp.bfloat16),
                pltpu.VMEM((row_count, channels, LANES), jnp.bfloat16),
                pltpu.VMEM((channels+BIAS_ROWS, row_count * LANES), jnp.bfloat16),
            ],
        ),
        input_output_aliases=aliases,
        compiler_params=pltpu.CompilerParams(vmem_limit_bytes=VMEM_BYTES),
        cost_estimate=pl.CostEstimate(flops=0, bytes_accessed=0, transcendentals=0),
        name="finish",
    )(place, *operands)


def add(a, b):
    return (a.astype(jnp.float32) + b.astype(jnp.float32)).astype(jnp.bfloat16)


NEAR = [(0, 1), (1, 0), (2, 3), (3, 2)]
FAR = [(0, 3), (3, 0), (1, 2), (2, 1)]


def sum_over_cols_axis(value):
    size = lax.axis_size("gy")
    if size & (size - 1):
        return lax.psum(value, "gy")
    step = 1
    while step < size:
        value = value + lax.ppermute(value, "gy", [(i, i ^ step) for i in range(size)])
        step *= 2
    return value


def body(
    plane_input, row_weight, col_weight, skip_weight, up_weight, up_bias, down_weight, down_bias
):
    channels, row_count, col_count = plane_input.shape
    mode_count = row_weight.shape[1]
    shares = lax.axis_size("gx")
    row_total = row_count * shares
    col_total = col_count * lax.axis_size("gy")
    row_scale = float(row_total * mode_count) ** (-0.5)
    col_scale = float(col_total * mode_count) ** (-0.5)
    share = lax.axis_index("gx")
    line = shares == 4
    inner = jnp.where((share == 1) | (share == 2), 1, 0) if line else jnp.zeros((), jnp.int32)
    place = jnp.stack([inner, 1 - inner, share]).astype(jnp.int32)
    blocks = col_count // LANES
    rounds = list(range(0, blocks, 2))
    tables = row_tables(mode_count, shares, row_count)

    partial = [row_modes(place, tables, plane_input, mode_count, base) for base in rounds]
    if line:
        near = [lax.ppermute(send, "gx", NEAR) for send, _ in partial]
        half = [add(keep, got) for (_, keep), got in zip(partial, near)]
    else:
        own = [lax.psum(keep.astype(jnp.float32), "gx").astype(jnp.bfloat16) for _, keep in partial]
        other = [lax.psum(send.astype(jnp.float32), "gx").astype(jnp.bfloat16) for send, _ in partial]

    row_mix, col_mix = mix_matrices(row_weight, col_weight)
    col_offset = lax.axis_index("gy") * col_count
    col_partial = col_modes(forward_table(mode_count, col_total, col_offset, col_count), plane_input)
    col_spectrum = sum_over_cols_axis(col_partial)
    if line:
        half[1], col_spectrum = lax.optimization_barrier((half[1], col_spectrum))
        far = [lax.ppermute(value, "gx", FAR) for value in half]
    col_spectrum = col_spectrum.astype(jnp.bfloat16).reshape(mode_count, 2 * channels, row_count)
    col_mixed = jnp.einsum(
        "koc,kcx->kox", col_mix, col_spectrum, preferred_element_type=jnp.float32
    )
    col_mixed = (col_mixed * col_scale).astype(jnp.bfloat16)
    col_mixed = col_mixed.reshape(2 * mode_count, channels, row_count).transpose(2, 1, 0)
    skip = jnp.broadcast_to(skip_weight.T[None], (row_count, channels, channels))
    local = jnp.concatenate([skip, col_mixed], axis=2)
    col_inverse = inverse_table(mode_count, col_total, col_offset, col_count)
    high = lax.reduce_precision(up_bias, 8, 7)
    middle = lax.reduce_precision(up_bias - high, 8, 7)
    low = up_bias - high - middle
    bias_part = jnp.pad(jnp.stack([high, middle, low], axis=1), ((0, 0), (0, BIAS_ROWS - 3)))
    bias_part = bias_part.astype(jnp.bfloat16)
    up = jnp.concatenate([up_weight.T, bias_part], axis=1)
    order = np.zeros((GROUP, GROUP, GROUP, GROUP), np.float32)
    for a in range(GROUP):
        for b in range(GROUP):
            order[a, b, b, a] = 1.0
    order = jnp.asarray(order.reshape(GROUP * GROUP, GROUP * GROUP), jnp.bfloat16)
    shared = (
        row_mix,
        row_inverse_tables(mode_count, shares, row_count),
        local,
        up,
        down_weight.T,
        jnp.broadcast_to(down_bias[:, None], (channels, LANES)),
        order,
    )
    out = None
    common = (shared, plane_input, col_inverse, row_scale)
    if line:
        waiting = []
        for i, base in enumerate(rounds):
            summed = half[i]
            if out is not None:
                summed, out = lax.optimization_barrier((summed, out))
            mine = add(summed, far[i])
            theirs = lax.ppermute(mine, "gx", NEAR)
            ready = waiting + [((base, 0), mine)]
            out = finish(place, [w[0] for w in ready], [w[1] for w in ready], *common, out)
            waiting = [((base, 1), theirs)]
        out = finish(place, [waiting[0][0]], [waiting[0][1]], *common, out)
    else:
        for base, mine, theirs in zip(rounds, own, other):
            out = finish(place, [(base, 0), (base, 1)], [mine, theirs], *common, out)
    return out


def solution(mesh):
    placed = (P(None, ("grp", "gx"), "gy"), P(), P(), P(), P(), P(), P(), P())
    return jax.shard_map(
        body, mesh=mesh, in_specs=placed, out_specs=P(None, ("grp", "gx"), "gy"), check_vma=False
    )
```

```python
import math

import jax
import jax.numpy as jnp
import numpy as np
from jax import lax
from jax.experimental import pallas as pl
from jax.experimental.pallas import tpu as pltpu
from jax.sharding import PartitionSpec as P

LANES = 128
GROUP = 16
HALF_GROUP = 8
BIAS_ROWS = 16
STEP_CHANNELS = 32
TILE = 512
VMEM_BYTES = 24 * 1024 * 1024
HEAD_VMEM_BYTES = 63 * 1024 * 1024

TAIL = 0.4
COEFFS = (0.15957266, 0.16051476, 0.12055834, 0.14408696, -0.08478078)
EXP_SCALE = -0.5 * math.log2(math.e)


def gelu(v):
    t = jnp.abs(v)
    s = pl.reciprocal(1.0 + TAIL * t, approx=True)
    poly = COEFFS[-1]
    for c in COEFFS[-2::-1]:
        poly = poly * s + c
    return jnp.maximum(v, 0.0) - jnp.exp2(t * t * EXP_SCALE) * (poly * s) * t


def row_tables(mode_count, shares, row_count):
    period = shares * row_count
    phases = np.arange(mode_count)[:, None] * np.arange(period)[None, :] % period
    angles = phases.astype(np.float64) * (2.0 * math.pi / period)
    table = np.stack([np.cos(angles), -np.sin(angles)], axis=1).reshape(2 * mode_count, shares, row_count)
    table = np.concatenate([table[:1], table[2:], table[1:2]], axis=0)
    eye = np.eye(HALF_GROUP)
    whole = np.einsum("jsx,cd->sjcdx", table, eye)
    return jnp.asarray(
        whole.reshape(shares, 2 * mode_count * HALF_GROUP, HALF_GROUP * row_count), jnp.bfloat16
    )


def row_inverse_tables(mode_count, shares, row_count):
    period = shares * row_count
    phases = np.arange(period)[:, None] * np.arange(mode_count)[None, :] % period
    angles = phases.astype(np.float64) * (2.0 * math.pi / period)
    factors = np.where(np.arange(mode_count) == 0, 1.0, 2.0)
    table = np.stack([factors * np.cos(angles), -factors * np.sin(angles)], axis=2)
    table = table.reshape(shares, row_count, 2 * mode_count)
    whole = np.einsum("sxj,cd->sxcjd", table, np.eye(GROUP))
    return jnp.asarray(
        whole.reshape(shares, row_count * GROUP, 2 * mode_count * GROUP), jnp.bfloat16
    )


def forward_table(mode_count, period, offset, number):
    wave_index = jnp.arange(mode_count, dtype=jnp.int32)
    cell_index = offset + jnp.arange(number, dtype=jnp.int32)
    phases = wave_index[:, None] * cell_index[None, :] % period
    angles = phases.astype(jnp.float32) * (2.0 * math.pi / period)
    both = jnp.stack([jnp.cos(angles), -jnp.sin(angles)], axis=1)
    return both.reshape(2 * mode_count, number).astype(jnp.bfloat16)


def inverse_table(mode_count, period, offset, number):
    wave_index = jnp.arange(mode_count, dtype=jnp.int32)
    cell_index = offset + jnp.arange(number, dtype=jnp.int32)
    phases = wave_index[:, None] * cell_index[None, :] % period
    angles = phases.astype(jnp.float32) * (2.0 * math.pi / period)
    factors = jnp.where(wave_index == 0, 1.0, 2.0).astype(jnp.float32)[:, None]
    both = jnp.stack([factors * jnp.cos(angles), -factors * jnp.sin(angles)], axis=1)
    return both.reshape(2 * mode_count, number).astype(jnp.bfloat16)


def mix_kernel(row_ref, col_ref, row_out_ref, col_out_ref):
    for source, target in ((row_ref, row_out_ref), (col_ref, col_out_ref)):
        for k in range(source.shape[1]):
            real = source[0, k].astype(jnp.float32).T
            imag = source[1, k].astype(jnp.float32).T
            upper = jnp.concatenate([real, -imag], axis=1)
            lower = jnp.concatenate([imag, real], axis=1)
            target[k] = jnp.concatenate([upper, lower], axis=0).astype(jnp.bfloat16)


def mix_matrices(row_weight, col_weight):
    _, modes, channels, _ = row_weight.shape
    shape = jax.ShapeDtypeStruct((modes, 2 * channels, 2 * channels), jnp.bfloat16)
    return pl.pallas_call(
        mix_kernel,
        out_shape=(shape, shape),
        compiler_params=pltpu.CompilerParams(vmem_limit_bytes=VMEM_BYTES),
        cost_estimate=pl.CostEstimate(flops=0, bytes_accessed=0, transcendentals=0),
        name="mix_matrices",
    )(row_weight, col_weight)


def row_modes_kernel(place_ref, table, *refs):
    for source, target in zip(refs[:2], refs[2:]):
        for g in range(source.shape[0] // GROUP):
            parts = []
            for half in range(2):
                first = g * GROUP + half * HALF_GROUP
                block = source[first : first + HALF_GROUP].reshape(-1, LANES)
                modes = jnp.dot(table[0], block, preferred_element_type=jnp.float32)
                parts.append(modes.reshape(-1, HALF_GROUP, LANES))
            at = slice(g * GROUP, (g + 1) * GROUP)
            target[:, at, :] = jnp.concatenate(parts, axis=1)[: target.shape[0]].astype(jnp.bfloat16)


def row_modes(place, tables, plane, mode_count, base):
    channels, row_count, _ = plane.shape
    modes = 2 * mode_count - 1
    groups = channels // STEP_CHANNELS
    shape = jax.ShapeDtypeStruct((modes, channels, LANES), jnp.bfloat16)
    block = pl.BlockSpec((modes, STEP_CHANNELS, LANES), lambda g, place: (0, g, 0))
    rows = tables.shape[1]

    table_at = pl.BlockSpec((1, rows, tables.shape[2]), lambda g, place: (place[2], 0, 0))

    def plane_at(which):
        return pl.BlockSpec(
            (STEP_CHANNELS, row_count, LANES),
            lambda g, place: (g, 0, base + place[which]),
        )

    return pl.pallas_call(
        row_modes_kernel,
        out_shape=(shape, shape),
        grid_spec=pltpu.PrefetchScalarGridSpec(
            num_scalar_prefetch=1,
            grid=(groups,),
            in_specs=[table_at, plane_at(1), plane_at(0)],
            out_specs=(block, block),
        ),
        compiler_params=pltpu.CompilerParams(vmem_limit_bytes=HEAD_VMEM_BYTES),
        cost_estimate=pl.CostEstimate(flops=0, bytes_accessed=0, transcendentals=0),
        name="row_modes",
    )(place, tables, plane, plane)


def col_modes_kernel(table_ref, plane_ref, out_ref):
    block = plane_ref[...].reshape(-1, plane_ref.shape[2])
    out_ref[...] = lax.dot_general(
        table_ref[...], block, (((1,), (1,)), ((), ())), preferred_element_type=jnp.float32
    )


def col_modes(table, plane):
    channels, row_count, col_count = plane.shape
    modes = table.shape[0]
    return pl.pallas_call(
        col_modes_kernel,
        out_shape=jax.ShapeDtypeStruct((modes, channels * row_count), jnp.float32),
        grid=(channels // GROUP,),
        in_specs=[
            pl.BlockSpec((modes, col_count), lambda g: (0, 0)),
            pl.BlockSpec((GROUP, row_count, col_count), lambda g: (g, 0, 0)),
        ],
        out_specs=pl.BlockSpec((modes, GROUP * row_count), lambda g: (0, g)),
        compiler_params=pltpu.CompilerParams(vmem_limit_bytes=HEAD_VMEM_BYTES),
        cost_estimate=pl.CostEstimate(flops=0, bytes_accessed=0, transcendentals=0),
        name="col_modes",
    )(table, plane)


def finish_kernel(
    row_scale,
    single,
    place_ref,
    modes_ref,
    more_ref,
    mix_ref,
    inverse_ref,
    local_ref,
    plane_ref,
    col_ref,
    up_ref,
    down_ref,
    down_bias_ref,
    order_ref,
    *rest,
):
    out_ref, mixed_ref, pre_ref, done_ref, rows_ref, wide_ref = rest[-6:]
    mode_rows, channels, _ = mixed_ref.shape
    row_count = plane_ref.shape[1]

    def mix(source):
        for k in range(mode_rows // 2):
            if k:
                pair = source[2 * k - 1 : 2 * k + 1].reshape(2 * channels, LANES)
                mixed = jnp.dot(mix_ref[k], pair, preferred_element_type=jnp.float32)
            else:
                mixed = jnp.dot(mix_ref[0, :, :channels], source[0], preferred_element_type=jnp.float32)
            mixed = (mixed * row_scale).astype(jnp.bfloat16)
            mixed_ref[2 * k : 2 * k + 2] = mixed.reshape(2, channels, LANES)

    if single:
        mix(modes_ref)
    else:
        pl.when(pl.program_id(0) == 0)(lambda: mix(modes_ref))
        pl.when(pl.program_id(0) == 1)(lambda: mix(more_ref))
    for g in range(channels // GROUP):
        for h in range(row_count // GROUP):
            o, x = slice(g * GROUP, (g + 1) * GROUP), slice(h * GROUP, (h + 1) * GROUP)
            block = plane_ref[o, x, :].reshape(GROUP * GROUP, LANES)
            turned = jnp.dot(order_ref[...], block, preferred_element_type=jnp.float32)
            rows_ref[x, o, :] = turned.astype(jnp.bfloat16).reshape(GROUP, GROUP, LANES)
    for g in range(channels // GROUP):
        part = mixed_ref[:, g * GROUP : (g + 1) * GROUP, :].reshape(mode_rows * GROUP, LANES)
        rows = jnp.dot(inverse_ref[0], part, preferred_element_type=jnp.float32)
        pre_ref[:, g * GROUP : (g + 1) * GROUP, :] = rows.reshape(row_count, GROUP, LANES)
    cols = col_ref[...]

    def one_row(x):
        data = jnp.concatenate([rows_ref[x], cols], axis=0)
        local = jnp.dot(local_ref[x], data, preferred_element_type=jnp.float32)
        return (pre_ref[x] + local).astype(jnp.bfloat16)

    def gather(x, carry):
        at = pl.ds(pl.multiple_of(x * LANES, LANES), LANES)
        wide_ref[:channels, at] = one_row(x)
        return carry

    lax.fori_loop(0, row_count, gather, 0, unroll=32)
    wide_ref[channels:, :] = jnp.ones((BIAS_ROWS, wide_ref.shape[1]), jnp.bfloat16)
    bias = down_bias_ref[...]
    tiles = wide_ref.shape[1] // TILE

    def up(i):
        return jnp.dot(up_ref[...], wide_ref[:, i * TILE : (i + 1) * TILE], preferred_element_type=jnp.float32)

    def down(i, hidden):
        out = jnp.dot(down_ref[...], hidden, preferred_element_type=jnp.float32)
        for q in range(TILE // LANES):
            done_ref[i * (TILE // LANES) + q] = (out[:, q * LANES : (q + 1) * LANES] + bias).astype(jnp.bfloat16)

    waiting = up(0)
    hidden = None
    for i in range(tiles):
        following = up(i + 1) if i + 1 < tiles else None
        active = gelu(waiting).astype(jnp.bfloat16)
        if hidden is not None:
            down(i - 1, hidden)
        hidden, waiting = active, following
    down(tiles - 1, hidden)
    for g in range(channels // GROUP):
        for h in range(row_count // GROUP):
            o, x = slice(g * GROUP, (g + 1) * GROUP), slice(h * GROUP, (h + 1) * GROUP)
            block = done_ref[x, o, :].reshape(GROUP * GROUP, LANES)
            turned = jnp.dot(order_ref[...], block, preferred_element_type=jnp.float32)
            out_ref[o, x, :] = turned.astype(jnp.bfloat16).reshape(GROUP, GROUP, LANES)


def finish(place, at, modes, shared, plane, col_inverse, row_scale, out):
    mix, inverse, local, up, down, down_bias, order = shared
    single = len(modes) == 1
    modes, more = modes[0], modes[-1]
    mode_rows = modes.shape[0] + 1

    def column(i, place):
        (base, which), (last_base, last_which) = at[0], at[-1]
        first = base + place[which]
        return first if single else jnp.where(i == 0, first, last_base + place[last_which])

    channels, row_count, col_count = plane.shape

    def whole(a):
        return pl.BlockSpec(a.shape, lambda i, place: (0,) * a.ndim)

    operands = [modes, more, mix, inverse, local, plane, col_inverse, up, down, down_bias, order]
    in_specs = [
        whole(modes),
        pl.BlockSpec(memory_space=pl.ANY) if single else whole(more),
        whole(mix),
        pl.BlockSpec((1,) + inverse.shape[1:], lambda i, place: (place[2], 0, 0)),
        whole(local),
        pl.BlockSpec((channels, row_count, LANES), lambda i, place: (0, 0, column(i, place))),
        pl.BlockSpec((col_inverse.shape[0], LANES), lambda i, place: (0, column(i, place))),
        whole(up),
        whole(down),
        whole(down_bias),
        whole(order),
    ]
    aliases = {}
    if out is not None:
        operands.append(out)
        in_specs.append(pl.BlockSpec(memory_space=pl.ANY))
        aliases = {len(operands): 0}

    def kernel(*refs):
        finish_kernel(row_scale, single, *refs)

    return pl.pallas_call(
        kernel,
        out_shape=jax.ShapeDtypeStruct((channels, row_count, col_count), jnp.bfloat16),
        grid_spec=pltpu.PrefetchScalarGridSpec(
            num_scalar_prefetch=1,
            grid=(1 if single else 2,),
            in_specs=in_specs,
            out_specs=pl.BlockSpec((channels, row_count, LANES), lambda i, place: (0, 0, column(i, place))),
            scratch_shapes=[
                pltpu.VMEM((mode_rows, channels, LANES), jnp.bfloat16),
                pltpu.VMEM((row_count, channels, LANES), jnp.float32),
                pltpu.VMEM((row_count, channels, LANES), jnp.bfloat16),
                pltpu.VMEM((row_count, channels, LANES), jnp.bfloat16),
                pltpu.VMEM((channels+BIAS_ROWS, row_count * LANES), jnp.bfloat16),
            ],
        ),
        input_output_aliases=aliases,
        compiler_params=pltpu.CompilerParams(vmem_limit_bytes=VMEM_BYTES),
        cost_estimate=pl.CostEstimate(flops=0, bytes_accessed=0, transcendentals=0),
        name="finish",
    )(place, *operands)


def add(a, b):
    return (a.astype(jnp.float32) + b.astype(jnp.float32)).astype(jnp.bfloat16)


NEAR = [(0, 1), (1, 0), (2, 3), (3, 2)]
FAR = [(0, 3), (3, 0), (1, 2), (2, 1)]


def sum_over_cols_axis(value):
    size = lax.axis_size("gy")
    if size & (size - 1):
        return lax.psum(value, "gy")
    step = 1
    while step < size:
        value = value + lax.ppermute(value, "gy", [(i, i ^ step) for i in range(size)])
        step *= 2
    return value


def body(
    plane_input, row_weight, col_weight, skip_weight, up_weight, up_bias, down_weight, down_bias
):
    channels, row_count, col_count = plane_input.shape
    mode_count = row_weight.shape[1]
    shares = lax.axis_size("gx")
    row_total = row_count * shares
    col_total = col_count * lax.axis_size("gy")
    row_scale = float(row_total * mode_count) ** (-0.5)
    col_scale = float(col_total * mode_count) ** (-0.5)
    share = lax.axis_index("gx")
    line = shares == 4
    inner = jnp.where((share == 1) | (share == 2), 1, 0) if line else jnp.zeros((), jnp.int32)
    place = jnp.stack([inner, 1 - inner, share]).astype(jnp.int32)
    blocks = col_count // LANES
    rounds = list(range(0, blocks, 2))
    tables = row_tables(mode_count, shares, row_count)

    partial = [row_modes(place, tables, plane_input, mode_count, base) for base in rounds]
    if line:
        near = [lax.ppermute(send, "gx", NEAR) for send, _ in partial]
        half = [add(keep, got) for (_, keep), got in zip(partial, near)]
    else:
        own = [lax.psum(keep.astype(jnp.float32), "gx").astype(jnp.bfloat16) for _, keep in partial]
        other = [lax.psum(send.astype(jnp.float32), "gx").astype(jnp.bfloat16) for send, _ in partial]

    row_mix, col_mix = mix_matrices(row_weight, col_weight)
    col_offset = lax.axis_index("gy") * col_count
    col_partial = col_modes(forward_table(mode_count, col_total, col_offset, col_count), plane_input)
    col_spectrum = sum_over_cols_axis(col_partial)
    if line:
        half[1], col_spectrum = lax.optimization_barrier((half[1], col_spectrum))
        far = [lax.ppermute(value, "gx", FAR) for value in half]
    col_spectrum = col_spectrum.astype(jnp.bfloat16).reshape(mode_count, 2 * channels, row_count)
    col_mixed = jnp.einsum(
        "koc,kcx->kox", col_mix, col_spectrum, preferred_element_type=jnp.float32
    )
    col_mixed = (col_mixed * col_scale).astype(jnp.bfloat16)
    col_mixed = col_mixed.reshape(2 * mode_count, channels, row_count).transpose(2, 1, 0)
    skip = jnp.broadcast_to(skip_weight.T[None], (row_count, channels, channels))
    local = jnp.concatenate([skip, col_mixed], axis=2)
    col_inverse = inverse_table(mode_count, col_total, col_offset, col_count)
    high = lax.reduce_precision(up_bias, 8, 7)
    middle = lax.reduce_precision(up_bias - high, 8, 7)
    low = up_bias - high - middle
    bias_part = jnp.pad(jnp.stack([high, middle, low], axis=1), ((0, 0), (0, BIAS_ROWS - 3)))
    bias_part = bias_part.astype(jnp.bfloat16)
    up = jnp.concatenate([up_weight.T, bias_part], axis=1)
    order = np.zeros((GROUP, GROUP, GROUP, GROUP), np.float32)
    for a in range(GROUP):
        for b in range(GROUP):
            order[a, b, b, a] = 1.0
    order = jnp.asarray(order.reshape(GROUP * GROUP, GROUP * GROUP), jnp.bfloat16)
    shared = (
        row_mix,
        row_inverse_tables(mode_count, shares, row_count),
        local,
        up,
        down_weight.T,
        jnp.broadcast_to(down_bias[:, None], (channels, LANES)),
        order,
    )
    out = None
    common = (shared, plane_input, col_inverse, row_scale)
    if line:
        waiting = []
        for i, base in enumerate(rounds):
            summed = half[i]
            if out is not None:
                summed, out = lax.optimization_barrier((summed, out))
            mine = add(summed, far[i])
            theirs = lax.ppermute(mine, "gx", NEAR)
            ready = waiting + [((base, 0), mine)]
            out = finish(place, [w[0] for w in ready], [w[1] for w in ready], *common, out)
            waiting = [((base, 1), theirs)]
        out = finish(place, [waiting[0][0]], [waiting[0][1]], *common, out)
    else:
        for base, mine, theirs in zip(rounds, own, other):
            out = finish(place, [(base, 0), (base, 1)], [mine, theirs], *common, out)
    return out


def solution(mesh):
    placed = (P(None, ("grp", "gx"), "gy"), P(), P(), P(), P(), P(), P(), P())
    return jax.shard_map(
        body, mesh=mesh, in_specs=placed, out_specs=P(None, ("grp", "gx"), "gy"), check_vma=False
    )
```
